32 devices in a mesh: groups: 2 (over x), dom: 8 (over z, y), mp: 2 (over core).
Axes of the slice: x: 2, y: 2, z: 4, core: 2. Of those that a mesh axis runs over, the one named last changes fastest.
Arguments:
- feats: bfloat16 [24576, 256], P(('groups', 'dom')), parts along dimension 0, may hold values from -6 to 6
- cell_count: int32 [16], P(('groups', 'dom')), parts along dimension 0, may hold values from 1 to 1536, 9216 in all
- tile_col: int32 [192, 8], P(('groups', 'dom')), parts along dimension 0, may hold values from 0 to 11, all different within a row
- tile_val: bfloat16 [192, 8, 128, 128], P(('groups', 'dom')), parts along dimension 0, may hold values from -0.1875 to 0.1875
- send_list: int32 [16, 8, 64], P(('groups', 'dom')), parts along dimension 0, may hold values from 0 to 1535
- send_count: int32 [16, 8], P(('groups', 'dom')), parts along dimension 0, may hold values from 1 to 64, 256 in all within a row
- recv_list: int32 [16, 8, 64], P(('groups', 'dom')), parts along dimension 0, may hold values from 0 to 1535
- gate_weight_matrix: bfloat16 [2, 256, 512], P(None, None, 'mp'), may hold values from -0.375 to 0.375
- w_up: bfloat16 [2, 256, 512], P(None, None, 'mp'), may hold values from -0.375 to 0.375
- w_down: bfloat16 [2, 512, 256], P(None, 'mp'), may hold values from -0.25 to 0.25
- out_grad: bfloat16 [24576, 256], P(('groups', 'dom')), parts along dimension 0, may hold values from -6 to 6
Outputs:
- final: bfloat16 [24576, 256], P(('groups', 'dom')), parts along dimension 0
- feat_grad: float32 [24576, 256], P(('groups', 'dom')), parts along dimension 0
- grad_gate: float32 [4, 256, 512], P('groups', None, 'mp'), parts along dimension 0
- grad_up: float32 [4, 256, 512], P('groups', None, 'mp'), parts along dimension 0
- down_weight_gradient: float32 [4, 512, 256], P('groups', 'mp'), parts along dimension 0
The draws below stay inside these ranges and needn't reach their ends.
There are 2 independent parts, one for each index of `groups`. The reference program is written for one: setup_inputs(seed, part) draws one part's arguments, and reference() takes and returns one part's arrays. A program takes and returns all parts, laid end to end along the dimension named above; an argument that names none is the same for every part. Nothing has to cross between parts.
Inputs may be any that keep to these rules, and one draw needn't show every extreme that they name: Partition p has live cells in its rows 0 to cell_count[p] - 1; some partition is full in every draw, and the counts sum to 9216. `tile_col`: the entries of one row block are distinct local block columns; every block column is named somewhere. `send_list`: slots at or past send_count are unused. `send_count`: entry [s, q] counts live slots from partition s to partition q, its own included; each row sums to 256 and its largest entry is exactly 64. `recv_list`: entry [q, s, k] is the receiver's local row fed by slot k from partition s.
All inputs are finite; a program needn't handle non-finite values. No bound on the sum of `cell_count` on one device may be relied on, other than what follows from the above.
Results may differ from the reference program's by a relative error of at most 0.03.
Values may be sent and summed in bfloat16 or wider, within the bound.
A program may use at most 128 MiB of HBM per device.

```python
import math
import jax
import jax.numpy as jnp
import numpy as np
from jax import lax

F = 256
H = 512
C_DEV = 1536
NB = 8
CAP = 64
L = 2
CELLS = 12288
N_DOM = 8


def place_ends(drawn, key, least, top_value):
    index_at = [jax.random.randint(jax.random.fold_in(key, axis), (), 0, length) for axis, length in enumerate(drawn.shape)]
    longest = drawn.shape.index(max(drawn.shape))
    beside = index_at[:longest] + [(index_at[longest] + 1) % drawn.shape[longest]] + index_at[longest + 1:]
    return drawn.at[tuple(index_at)].set(least).at[tuple(beside)].set(top_value)


def block_scale(own_key, dims, shards, least, top_value):
    def one(dim, blocks):
        draws = jax.random.uniform(jax.random.fold_in(jax.random.fold_in(own_key, 6), dim), (blocks,), jnp.float32, least / len(shards), top_value / len(shards))
        return jnp.repeat(jnp.exp(draws), dims[dim] // blocks).reshape((-1,) + (1,) * (len(dims) - dim - 1))

    loudness = one(*shards[0])
    for cut in shards[1:]:
        loudness = loudness * one(*cut)
    return loudness


def picks_of(own_key, rows, number_of, top, lift):
    sequence = jax.random.permutation(jax.random.fold_in(own_key, 1), number_of)
    favour = sequence
    for power in range(3):
        favour = favour * favour // number_of
    favour = favour * lift // number_of
    chance = jax.random.randint(jax.random.fold_in(own_key, 2), (rows, number_of), 0, 4096) + favour
    sure = jax.random.permutation(jax.random.fold_in(own_key, 3), rows)[jnp.arange(number_of) % rows]
    chance = jnp.where(jnp.arange(rows)[:, None] == sure[None, :], 1 << 14, chance)
    merit = chance * number_of + jnp.arange(number_of)
    return lax.top_k(merit.astype(jnp.int32), top)[1].astype(jnp.int32)


def profile(number_of, total, reach, lean):
    loads = [(1 << 20) // math.isqrt(rank ** lean) + 1 for rank in range(2, number_of + 1)]
    surplus, counts = total - reach - (number_of - 1), [1] * (number_of - 1)
    while surplus > 0:
        candidates = [i for i in range(number_of - 1) if counts[i] < reach]
        mass, remaining = sum([loads[i] for i in candidates]), surplus
        for i in candidates:
            extra = min(reach - counts[i], max(1, remaining * loads[i] // mass), surplus)
            counts[i] = counts[i] + extra
            surplus = surplus - extra
    return np.array([reach] + counts)


def ragged_sizes(own_key, count, total, most, skew):
    if count == 2:
        one = jax.random.randint(own_key, (), max(1, total - most), min(most, total - 1) + 1)
        return jnp.stack([one, total - one])
    sizes = jnp.asarray(profile(count, total, most, skew), jnp.int32)
    twos = (count - 1) // 2
    donor, receiver = sizes[1:1 + 2 * twos:2], sizes[2:2 + 2 * twos:2]
    margin = jnp.minimum(donor - 1, most - receiver)
    moved = jax.random.randint(jax.random.fold_in(own_key, 1), (twos,), 0, 1 << 20) % (margin + 1)
    sizes = sizes.at[1:1 + 2 * twos:2].set(donor - moved).at[2:2 + 2 * twos:2].set(receiver + moved)
    return sizes[jax.random.permutation(jax.random.fold_in(own_key, 2), count)]


def scatter_about(stream_key, extent, spread, reach, split=(), held_as=jnp.bfloat16):
    factor_of = block_scale(stream_key, extent, split, -0.22, 0.18) if split else 1.0
    result = jax.random.normal(stream_key, extent, jnp.float32) * spread * factor_of
    return jnp.minimum(jnp.maximum(result, -reach), reach).astype(held_as)


def setup_inputs(seed: int = 0, part: int = 0) -> dict:
    seeds = jax.random.split(jax.random.key(seed), 12)
    part_keys = jax.random.split(jax.random.fold_in(seeds[11], part), 12)
    return {
        "feats": scatter_about(part_keys[0], (CELLS, F), 1.0, 6.0, ((0, 8),)),
        "cell_count": ragged_sizes(part_keys[1], N_DOM, N_DOM * C_DEV * 3 // 4, C_DEV, 2).astype(jnp.int32),
        "tile_col": picks_of(part_keys[2], (CELLS // 128), C_DEV // 128, NB, 0),
        "tile_val": scatter_about(part_keys[3], (CELLS // 128, NB, 128, 128), (NB * 128) ** -0.5, 0.1875, ((0, 8),)),
        "send_list": place_ends(jax.random.randint(part_keys[4], (N_DOM, N_DOM, CAP), 0, C_DEV), jax.random.fold_in(part_keys[4], 1), 0, C_DEV - 1).astype(jnp.int32),
        "send_count": jax.vmap(lambda own: ragged_sizes(own, N_DOM, N_DOM * CAP // 2, CAP, 2))(jax.random.split(part_keys[5], N_DOM)).reshape((N_DOM, N_DOM)).astype(jnp.int32),
        "recv_list": place_ends(jax.random.randint(part_keys[6], (N_DOM, N_DOM, CAP), 0, C_DEV), jax.random.fold_in(part_keys[6], 1), 0, C_DEV - 1).astype(jnp.int32),
        "gate_weight_matrix": scatter_about(seeds[7], (L, F, H), F ** -0.5, 0.375, ((2, 2),)),
        "w_up": scatter_about(seeds[8], (L, F, H), F ** -0.5, 0.375, ((2, 2),)),
        "w_down": scatter_about(seeds[9], (L, H, F), H ** -0.5, 0.25, ((1, 2),)),
        "out_grad": scatter_about(part_keys[10], (CELLS, F), 1.0, 6.0, ((0, 8),)),
    }


def gate_terms(gate_pre):
    sigmoid = jax.nn.sigmoid(gate_pre)
    return gate_pre * sigmoid, sigmoid * (1.0 + gate_pre * (1.0 - sigmoid))


def local_forward(current, tile_col, tile_val):
    block_count = C_DEV // 128
    blocks = current.reshape(N_DOM, block_count, 128, F)
    tiles = tile_val.reshape(N_DOM, block_count, NB, 128, 128)
    columns = tile_col.reshape(N_DOM, block_count, NB)

    def one_part(operands):
        block_rows, partition_tile_rows, part_cols = operands
        picked = block_rows[part_cols]
        summed_messages = jnp.einsum("rjab,rjbf->raf", partition_tile_rows.astype(jnp.float32), picked.astype(jnp.float32))
        return summed_messages.reshape(C_DEV, F)

    return lax.map(one_part, (blocks, tiles, columns))


def local_backward(upstream, tile_col, tile_val):
    block_count = C_DEV // 128
    blocks = upstream.reshape(N_DOM, block_count, 128, F)
    tiles = tile_val.reshape(N_DOM, block_count, NB, 128, 128)
    columns = tile_col.reshape(N_DOM, block_count, NB)

    def one_part(operands):
        block_rows, partition_tile_rows, part_cols = operands
        contribution_part = jnp.einsum("rjab,raf->rjbf", partition_tile_rows.astype(jnp.float32), block_rows.astype(jnp.float32))
        summed_messages = jnp.zeros((block_count, 128, F), jnp.float32).at[part_cols.reshape(-1)].add(
            contribution_part.reshape(block_count * NB, 128, F))
        return summed_messages.reshape(C_DEV, F)

    return lax.map(one_part, (blocks, tiles, columns))


def slot_live(send_count):
    return (jnp.arange(CAP)[None, None, :] < send_count[:, :, None]).astype(jnp.float32)[..., None]


def halo_forward(current, send_list, send_count, recv_list):
    sender = jnp.arange(N_DOM)[:, None, None]
    leaving = current[sender, send_list].astype(jnp.float32) * slot_live(send_count)
    arriving = jnp.swapaxes(leaving, 0, 1)
    flat_target = (sender * C_DEV + recv_list).astype(jnp.int32).reshape(-1)
    summed_messages = jnp.zeros((N_DOM * C_DEV, F), jnp.float32).at[flat_target].add(arriving.reshape(-1, F))
    return summed_messages.reshape(N_DOM, C_DEV, F)


def halo_backward(upstream, send_list, send_count, recv_list):
    owner = jnp.arange(N_DOM)[:, None, None]
    flat_target = (owner * C_DEV + recv_list).astype(jnp.int32).reshape(-1)
    picked = upstream.reshape(N_DOM * C_DEV, F)[flat_target].reshape(N_DOM, N_DOM, CAP, F).astype(jnp.float32)
    returning = jnp.swapaxes(picked, 0, 1) * slot_live(send_count)
    flat_source = (owner * C_DEV + send_list).astype(jnp.int32).reshape(-1)
    summed_messages = jnp.zeros((N_DOM * C_DEV, F), jnp.float32).at[flat_source].add(returning.reshape(-1, F))
    return summed_messages.reshape(N_DOM, C_DEV, F)


def reference(feats, cell_count, tile_col, tile_val, send_list, send_count, recv_list, gate_weight_matrix, w_up, w_down, out_grad):
    live_mask = (jnp.arange(C_DEV)[None, :] < cell_count[:, None]).astype(jnp.float32)[..., None]
    current = (feats.reshape(N_DOM, C_DEV, F).astype(jnp.float32) * live_mask).astype(jnp.bfloat16)
    stored = []
    for layer_index in range(L):
        summed_messages = local_forward(current, tile_col, tile_val) + halo_forward(current, send_list, send_count, recv_list)
        acts = summed_messages.astype(jnp.bfloat16).reshape(CELLS, F)
        gate_pre = jnp.dot(acts, gate_weight_matrix[layer_index], preferred_element_type=jnp.float32)
        up_preactivation = jnp.dot(acts, w_up[layer_index], preferred_element_type=jnp.float32)
        silu_value, silu_slope = gate_terms(gate_pre)
        hidden = (silu_value * up_preactivation).astype(jnp.bfloat16)
        mixed = jnp.dot(hidden, w_down[layer_index], preferred_element_type=jnp.float32).reshape(N_DOM, C_DEV, F)
        stored.append((acts, up_preactivation, silu_value, silu_slope, hidden))
        current = ((current.astype(jnp.float32) + mixed) * live_mask).astype(jnp.bfloat16)
    final = current.reshape(CELLS, F)
    carried = out_grad.reshape(N_DOM, C_DEV, F).astype(jnp.float32)
    grad_gates, up_weight_gradients, grad_downs = [], [], []
    for layer_index in reversed(range(L)):
        acts, up_preactivation, silu_value, silu_slope, hidden = stored[layer_index]
        upstream = carried * live_mask
        down_in = upstream.astype(jnp.bfloat16).reshape(CELLS, F)
        grad_downs.append(jnp.dot(hidden.T, down_in, preferred_element_type=jnp.float32))
        hidden_grad = jnp.dot(down_in, w_down[layer_index].T, preferred_element_type=jnp.float32)
        gate_grad = (hidden_grad * up_preactivation * silu_slope).astype(jnp.bfloat16)
        up_grad = (hidden_grad * silu_value).astype(jnp.bfloat16)
        grad_gates.append(jnp.dot(acts.T, gate_grad, preferred_element_type=jnp.float32))
        up_weight_gradients.append(jnp.dot(acts.T, up_grad, preferred_element_type=jnp.float32))
        agg_grad = (jnp.dot(gate_grad, gate_weight_matrix[layer_index].T, preferred_element_type=jnp.float32)
                    + jnp.dot(up_grad, w_up[layer_index].T, preferred_element_type=jnp.float32)).astype(jnp.bfloat16)
        agg_grad = agg_grad.reshape(N_DOM, C_DEV, F)
        carried = upstream + local_backward(agg_grad, tile_col, tile_val) + halo_backward(
            agg_grad, send_list, send_count, recv_list)
    feat_grad = (carried * live_mask).reshape(CELLS, F)
    grad_gate = jnp.stack(grad_gates[::-1])
    grad_up = jnp.stack(up_weight_gradients[::-1])
    down_weight_gradient = jnp.stack(grad_downs[::-1])
    return (final, feat_grad, grad_gate, grad_up, down_weight_gradient)
```

```python
import functools

import jax
import jax.numpy as jnp
from jax import lax
from jax.experimental import pallas as pl
from jax.experimental.pallas import tpu as pltpu
from jax.sharding import PartitionSpec as P

MESH = pl.DeviceIdType.MESH
BLOCK = 128
LANES = 128
TILE = 256


def dot_nn(left, right):
    return lax.dot_general(
        left, right, (((1,), (0,)), ((), ())), preferred_element_type=jnp.float32
    )


def dot_nt(left, right):
    return lax.dot_general(
        left, right, (((1,), (1,)), ((), ())), preferred_element_type=jnp.float32
    )


def dot_tn(left, right):
    return lax.dot_general(
        left, right, (((0,), (0,)), ((), ())), preferred_element_type=jnp.float32
    )


def remote(src, dst, send_sem, recv_sem, dom, core):
    return pltpu.make_async_remote_copy(
        src_ref=src,
        dst_ref=dst,
        send_sem=send_sem,
        recv_sem=recv_sem,
        device_id={"dom": dom, "mp": core},
        device_id_type=MESH,
    )


def aligned(index, size):
    return pl.ds(pl.multiple_of(index * size, size), size)


def kernel(
    parts,
    inv_ref,
    count_ref,
    idx_ref,
    feats_ref,
    tiles_ref,
    cot_ref,
    wg_in,
    wu_in,
    wd_in,
    final_ref,
    fg_ref,
    gg_out,
    gu_out,
    gd_out,
    adj,
    adj_t,
    own_pick,
    s_t,
    r_t,
    states,
    acts,
    hid,
    pre_g,
    pre_u,
    down_in,
    agg_grad,
    wg,
    wu,
    wd,
    sbuf,
    halo,
    grads,
    res,
    p_one,
    p_sum,
    p_two,
    q_one,
    q_sum,
    q_two,
    h_send,
    h_recv,
    f_send,
    f_recv,
    w_send,
    w_recv,
    a_send,
    a_recv,
):
    me = lax.axis_index("dom")
    core = lax.axis_index("mp")
    sib = 1 - core
    layers = wg_in.shape[0]
    width = feats_ref.shape[1]
    units = wg_in.shape[2]
    rows = feats_ref.shape[0]
    blocks = rows // BLOCK
    tiles = rows // TILE
    slots = sbuf.shape[2]
    outer = parts // 2
    y = lax.rem(me, 2)
    z = me // 2
    f32, bf16 = jnp.float32, jnp.bfloat16

    barrier = pltpu.get_barrier_semaphore()

    def greet(i, _):
        q = lax.rem(me + i, parts)
        pl.semaphore_signal(
            barrier, inc=1, device_id={"dom": q, "mp": core}, device_id_type=MESH
        )
        return 0

    lax.fori_loop(1, parts, greet, 0)
    pl.semaphore_signal(barrier, inc=1, device_id={"dom": me, "mp": sib}, device_id_type=MESH)

    count = count_ref[0]

    def mask_of(i):
        index = lax.broadcasted_iota(jnp.int32, (TILE, 1), 0) + i * TILE
        return (index < count).astype(f32)

    def mask_rows(i, _):
        at = aligned(i, TILE)
        states[0, at, :] = (feats_ref[at, :].astype(f32) * mask_of(i)).astype(bf16)
        return 0

    lax.fori_loop(0, tiles, mask_rows, 0)

    columns = jnp.transpose(idx_ref[...])
    own_rows = parts * slots
    own_cols = jnp.where(core == 0, columns[:own_rows], columns[own_rows:])
    step = min(own_rows, TILE)
    for begin in range(0, own_rows, step):
        lane = lax.broadcasted_iota(jnp.int32, (step, rows), 1)
        own_pick[begin : begin + step, :] = (own_cols[begin : begin + step, 0:1] == lane).astype(
            f32
        ).astype(bf16)

    pl.semaphore_wait(barrier, parts)

    def halo_send(phase, onehot, source):
        for begin in range(0, own_rows, step):
            picked = dot_nn(onehot[begin : begin + step, :], source[...]).astype(bf16)
            sbuf[phase, begin // slots : (begin + step) // slots] = picked.reshape(
                step // slots, slots, width
            )
        halo[phase, core, me] = sbuf[phase, me]

        def send(i, _):
            q = lax.rem(me + i, parts)
            remote(
                sbuf.at[phase, q],
                halo.at[phase, core, me],
                h_send.at[phase, q],
                h_recv.at[phase, me],
                q,
                core,
            ).start()
            return 0

        lax.fori_loop(1, parts, send, 0)
        forward(phase, me).start()

    def forward(phase, s):
        return remote(
            halo.at[phase, core, s],
            halo.at[phase, core, s],
            f_send.at[phase, s],
            f_recv.at[phase, s],
            me,
            sib,
        )

    def arrival(phase, s):
        return remote(
            sbuf.at[phase, s],
            halo.at[phase, core, s],
            h_send.at[phase, s],
            h_recv.at[phase, s],
            s,
            core,
        )

    def halo_recv(phase):
        def take(i, _):
            s = lax.rem(me + parts - i, parts)
            arrival(phase, s).wait_recv()
            forward(phase, s).start()
            return 0

        lax.fori_loop(1, parts, take, 0)

        def settle(s, _):
            remote(
                halo.at[phase, sib, s],
                halo.at[phase, sib, s],
                f_send.at[phase, s],
                f_recv.at[phase, s],
                me,
                sib,
            ).wait_recv()
            return 0

        lax.fori_loop(0, parts, settle, 0)

    def landed_rows(phase):
        return halo[phase].reshape(2 * own_rows, width)

    halo_send(0, own_pick, states.at[0])

    weight_copies = []
    for k, (src, dst) in enumerate(((wg_in, wg), (wu_in, wu), (wd_in, wd))):
        copy = remote(src, dst.at[core], w_send.at[k], w_recv.at[k], me, sib)
        copy.start()
        weight_copies.append(copy)
        dst[core] = src[...]

    def build(r, _):
        for c in range(blocks):
            j = inv_ref[r, c]
            tile = tiles_ref[r, jnp.maximum(j, 0)]
            adj[aligned(r, BLOCK), c * BLOCK : (c + 1) * BLOCK] = jnp.where(
                j >= 0, tile, jnp.zeros_like(tile)
            )
        return 0

    lax.fori_loop(0, blocks, build, 0)

    def build_columns(i, _):
        at = aligned(i, TILE)
        index = lax.broadcasted_iota(jnp.int32, (TILE, 2 * own_rows), 0) + i * TILE
        s_t[at, :] = (idx_ref[0:1, :] == index).astype(f32).astype(bf16)
        r_t[at, :] = (idx_ref[1:2, :] == index).astype(f32).astype(bf16)
        return 0

    def build_back():
        for begin in range(0, own_rows, step):
            lane = lax.broadcasted_iota(jnp.int32, (step, rows), 1)
            own_pick[begin : begin + step, :] = (own_cols[begin : begin + step, 1:2] == lane).astype(
                f32
            ).astype(bf16)

    def turn_tiles():
        def turn(r, _):
            for c in range(blocks):
                adj_t[c * BLOCK : (c + 1) * BLOCK, aligned(r, BLOCK)] = jnp.transpose(
                    adj[aligned(r, BLOCK), c * BLOCK : (c + 1) * BLOCK]
                )
            return 0

        lax.fori_loop(0, blocks, turn, 0)

    for layer in range(layers):
        if layer:
            halo_send(layer, own_pick, states.at[layer])
        state = states.at[layer]

        def gather(i, _, state=state):
            at = aligned(i, TILE)
            fg_ref[at, :] = dot_nn(adj[at, :], state[...])
            return 0

        lax.fori_loop(0, tiles, gather, 0)
        if layer == 0:
            lax.fori_loop(0, tiles, build_columns, 0)
            turn_tiles()
            for copy in weight_copies:
                copy.wait_recv()
        if layer == layers - 1:
            build_back()
        halo_recv(layer)

        def mlp(i, _, layer=layer, state=state):
            at = aligned(i, TILE)
            act = (fg_ref[at, :] + dot_nn(r_t[at, :], landed_rows(layer))).astype(bf16)
            acts[layer, at, :] = act
            mixed = jnp.zeros((TILE, width), f32)
            for h in range(2):
                gate = dot_nn(act, wg[h, layer])
                up = dot_nn(act, wu[h, layer])
                sg = 0.5 * jnp.tanh(0.5 * gate) + 0.5
                silu = gate * sg
                hidden = (silu * up).astype(bf16)
                hid[layer, h, at, :] = hidden
                pre_g[layer, h, at, :] = (up * (sg * (1.0 + gate * (1.0 - sg)))).astype(bf16)
                pre_u[layer, h, at, :] = silu.astype(bf16)
                mixed = mixed + dot_nn(hidden, wd[h, layer])
            new = ((state[at, :].astype(f32) + mixed) * mask_of(i)).astype(bf16)
            if layer + 1 < layers:
                states[layer + 1, at, :] = new
            else:
                final_ref[at, :] = new
            return 0

        lax.fori_loop(0, tiles, mlp, 0)

    total = grads.shape[1]
    p_rows = total * 2 // 3
    p_half = p_rows // 2
    p_seg = p_half // outer
    q_seg = (total - p_rows) // outer
    q_half = q_seg // 2

    def at_rows(base, index, size):
        return pl.ds(pl.multiple_of(base + index * size, 16), size)

    def each_other(fn):
        def go(i, _):
            fn(lax.rem(z + i, outer))
            return 0

        lax.fori_loop(1, outer, go, 0)

    def pair(stage, layer, src, dst):
        return remote(
            src,
            dst,
            a_send.at[layer, stage, outer],
            a_recv.at[layer, stage, outer],
            z * 2 + 1 - y,
            core,
        )

    def line(stage, layer, src, dst, to, slot):
        return remote(
            src,
            dst,
            a_send.at[layer, stage, to],
            a_recv.at[layer, stage, slot],
            to * 2 + y,
            core,
        )

    def reduce_one(layer):
        pair(0, layer, grads.at[layer, at_rows(0, 1 - y, p_half)], p_one.at[layer]).start()
        each_other(
            lambda t: line(
                0,
                layer,
                grads.at[layer, at_rows(p_rows, t, q_seg)],
                q_one.at[layer, z],
                t,
                z,
            ).start()
        )
        q_one[layer, z] = grads[layer, at_rows(p_rows, z, q_seg)]

    def reduce_two(layer):
        pair(0, layer, grads.at[layer, at_rows(0, 1 - y, p_half)], p_one.at[layer]).wait_recv()
        p_sum[layer] = (
            grads[layer, at_rows(0, y, p_half)].astype(f32) + p_one[layer].astype(f32)
        ).astype(bf16)
        each_other(
            lambda t: line(
                1, layer, p_sum.at[layer, at_rows(0, t, p_seg)], p_two.at[layer, z], t, z
            ).start()
        )
        p_two[layer, z] = p_sum[layer, at_rows(0, z, p_seg)]
        each_other(
            lambda t: line(
                0,
                layer,
                grads.at[layer, at_rows(p_rows, t, q_seg)],
                q_one.at[layer, t],
                t,
                t,
            ).wait_recv()
        )
        q_sum[layer] = jnp.sum(q_one[layer].astype(f32), axis=0).astype(bf16)
        pair(1, layer, q_sum.at[layer, at_rows(0, 1 - y, q_half)], q_two.at[layer]).start()

    def reduce_three(layer):
        each_other(
            lambda t: line(
                1, layer, p_sum.at[layer, at_rows(0, t, p_seg)], p_two.at[layer, t], t, t
            ).wait_recv()
        )
        mine = at_rows(y * p_half, z, p_seg)
        res[layer, mine] = jnp.sum(p_two[layer].astype(f32), axis=0).astype(bf16)
        each_other(
            lambda t: line(2, layer, res.at[layer, mine], res.at[layer, mine], t, z).start()
        )
        pair(1, layer, q_sum.at[layer, at_rows(0, 1 - y, q_half)], q_two.at[layer]).wait_recv()
        own = at_rows(p_rows + z * q_seg, y, q_half)
        res[layer, own] = (
            q_sum[layer, at_rows(0, y, q_half)].astype(f32) + q_two[layer].astype(f32)
        ).astype(bf16)
        pair(2, layer, res.at[layer, own], res.at[layer, own]).start()

    def reduce_four(layer):
        def landed(t):
            there = at_rows(y * p_half, t, p_seg)
            line(2, layer, res.at[layer, there], res.at[layer, there], t, t).wait_recv()

        each_other(landed)
        half = at_rows(0, y, p_half)
        pair(3, layer, res.at[layer, half], res.at[layer, half]).start()
        other = at_rows(p_rows + z * q_seg, 1 - y, q_half)
        pair(2, layer, res.at[layer, other], res.at[layer, other]).wait_recv()
        own = at_rows(p_rows, z, q_seg)
        each_other(lambda t: line(3, layer, res.at[layer, own], res.at[layer, own], t, z).start())

    def reduce_end(layer):
        half = at_rows(0, 1 - y, p_half)
        pair(3, layer, res.at[layer, half], res.at[layer, half]).wait_recv()

        def landed(t):
            there = at_rows(p_rows, t, q_seg)
            line(3, layer, res.at[layer, there], res.at[layer, there], t, t).wait_recv()

        each_other(landed)
        at = 0
        for out in (gg_out, gu_out, gd_out):
            height, wide = out.shape[1:]
            for c in range(0, wide, LANES):
                out[layer, :, c : c + LANES] = res[layer, at : at + height].astype(f32)
                at += height

    def reduce_drain(layer):
        pair(0, layer, grads.at[layer, at_rows(0, 1 - y, p_half)], p_one.at[layer]).wait_send()
        pair(1, layer, q_sum.at[layer, at_rows(0, 1 - y, q_half)], q_two.at[layer]).wait_send()
        own = at_rows(p_rows + z * q_seg, y, q_half)
        pair(2, layer, res.at[layer, own], res.at[layer, own]).wait_send()
        half = at_rows(0, y, p_half)
        pair(3, layer, res.at[layer, half], res.at[layer, half]).wait_send()
        mine = at_rows(y * p_half, z, p_seg)
        whole = at_rows(p_rows, z, q_seg)

        def sent(t):
            line(
                0,
                layer,
                grads.at[layer, at_rows(p_rows, t, q_seg)],
                q_one.at[layer, z],
                t,
                z,
            ).wait_send()
            line(
                1, layer, p_sum.at[layer, at_rows(0, t, p_seg)], p_two.at[layer, z], t, z
            ).wait_send()
            line(2, layer, res.at[layer, mine], res.at[layer, mine], t, z).wait_send()
            line(3, layer, res.at[layer, whole], res.at[layer, whole], t, z).wait_send()

        each_other(sent)

    def start_rows(i, _):
        at = aligned(i, TILE)
        fg_ref[at, :] = cot_ref[at, :].astype(f32) * mask_of(i)
        return 0

    lax.fori_loop(0, tiles, start_rows, 0)

    for layer in reversed(range(layers)):
        phase = 2 * layers - 1 - layer
        last = layer == layers - 1

        def mlp_back(i, _, layer=layer):
            at = aligned(i, TILE)
            down = fg_ref[at, :].astype(bf16)
            down_in[at, :] = down
            total = jnp.zeros((TILE, width), f32)
            for h in range(2):
                hidden_grad = dot_nt(down, wd[h, layer])
                gate_grad = (hidden_grad * pre_g[layer, h, at, :].astype(f32)).astype(bf16)
                up_grad = (hidden_grad * pre_u[layer, h, at, :].astype(f32)).astype(bf16)
                pre_g[layer, h, at, :] = gate_grad
                pre_u[layer, h, at, :] = up_grad
                total = total + dot_nt(gate_grad, wg[h, layer]) + dot_nt(up_grad, wu[h, layer])
            agg_grad[at, :] = total.astype(bf16)
            return 0

        lax.fori_loop(0, tiles, mlp_back, 0)
        halo_send(phase, own_pick, agg_grad)
        if not last:
            reduce_three(layer + 1)

        at = 0
        act = acts[layer]
        for left, right in (
            (act, pre_g[layer, core]),
            (act, pre_u[layer, core]),
            (hid[layer, core], down_in[...]),
        ):
            part = dot_tn(left, right).astype(bf16)
            for c in range(0, part.shape[1], LANES):
                grads[layer, at : at + part.shape[0], :] = part[:, c : c + LANES]
                at += part.shape[0]
        reduce_one(layer)

        def gather_back(i, _):
            at = aligned(i, TILE)
            fg_ref[at, :] = fg_ref[at, :] + dot_nn(adj_t[at, :], agg_grad[...])
            return 0

        lax.fori_loop(0, tiles, gather_back, 0)
        if not last:
            reduce_four(layer + 1)
        halo_recv(phase)

        def finish(i, _, phase=phase):
            at = aligned(i, TILE)
            fg_ref[at, :] = (fg_ref[at, :] + dot_nn(s_t[at, :], landed_rows(phase))) * mask_of(i)
            return 0

        if last:
            lax.fori_loop(0, tiles, finish, 0)
            reduce_two(layer)
        else:
            reduce_two(layer)
            lax.fori_loop(0, tiles, finish, 0)
            reduce_end(layer + 1)

    reduce_three(0)
    reduce_four(0)
    reduce_end(0)
    for layer in range(layers):
        reduce_drain(layer)
    for copy in weight_copies:
        copy.wait_send()
    for phase in range(2 * layers):

        def drained(i, _, phase=phase):
            q = lax.rem(me + i, parts)
            arrival(phase, q).wait_send()
            forward(phase, q).wait_send()
            return 0

        lax.fori_loop(1, parts, drained, 0)
        forward(phase, me).wait_send()


def local(
    parts,
    feats,
    cell_count,
    tile_col,
    tile_val,
    send_list,
    send_count,
    recv_list,
    gate_weight_matrix,
    w_up,
    w_down,
    out_grad,
):
    rows, width = feats.shape
    layers, _, units = gate_weight_matrix.shape
    blocks, per_row = tile_col.shape
    slot_count = send_list.shape[2]
    half = slot_count // 2
    outer = parts // 2
    all_slots = parts * slot_count
    position = jnp.arange(1, per_row + 1, dtype=jnp.int32)[None, :, None]
    chosen = tile_col[:, :, None] == jnp.arange(blocks, dtype=jnp.int32)[None, None, :]
    inverse = jnp.sum(jnp.where(chosen, position, 0), axis=1) - 1
    live = jnp.arange(slot_count)[None, :] < send_count[0][:, None]
    listed = jnp.stack([jnp.where(live, send_list[0], -1), recv_list[0]])
    listed = jnp.swapaxes(listed.reshape(2, parts, 2, half), 1, 2).reshape(2, all_slots)
    listed = jnp.pad(listed, ((0, 6), (0, 0)))

    total = 2 * width * (units // LANES) + units * (width // LANES)
    p_half = total // 3
    q_seg = (total - 2 * p_half) // outer
    f32, bf16 = jnp.float32, jnp.bfloat16
    vmem = pl.BlockSpec(memory_space=pltpu.VMEM)
    smem = pl.BlockSpec(memory_space=pltpu.SMEM)
    phases = 2 * layers
    dma = pltpu.SemaphoreType.DMA
    return pl.pallas_call(
        functools.partial(kernel, parts),
        out_shape=(
            jax.ShapeDtypeStruct((rows, width), bf16),
            jax.ShapeDtypeStruct((rows, width), f32),
            jax.ShapeDtypeStruct((layers, width, units), f32),
            jax.ShapeDtypeStruct((layers, width, units), f32),
            jax.ShapeDtypeStruct((layers, units, width), f32),
        ),
        in_specs=[smem, smem] + [vmem] * 7,
        out_specs=[vmem] * 5,
        scratch_shapes=[
            pltpu.VMEM((rows, rows), bf16),
            pltpu.VMEM((rows, rows), bf16),
            pltpu.VMEM((all_slots // 2, rows), bf16),
            pltpu.VMEM((rows, all_slots), bf16),
            pltpu.VMEM((rows, all_slots), bf16),
            pltpu.VMEM((layers, rows, width), bf16),
            pltpu.VMEM((layers, rows, width), bf16),
            pltpu.VMEM((layers, 2, rows, units), bf16),
            pltpu.VMEM((layers, 2, rows, units), bf16),
            pltpu.VMEM((layers, 2, rows, units), bf16),
            pltpu.VMEM((rows, width), bf16),
            pltpu.VMEM((rows, width), bf16),
            pltpu.VMEM((2, layers, width, units), bf16),
            pltpu.VMEM((2, layers, width, units), bf16),
            pltpu.VMEM((2, layers, units, width), bf16),
            pltpu.VMEM((phases, parts, half, width), bf16),
            pltpu.VMEM((phases, 2, parts, half, width), bf16),
            pltpu.VMEM((layers, total, LANES), bf16),
            pltpu.VMEM((layers, total, LANES), bf16),
            pltpu.VMEM((layers, p_half, LANES), bf16),
            pltpu.VMEM((layers, p_half, LANES), bf16),
            pltpu.VMEM((layers, outer, p_half // outer, LANES), bf16),
            pltpu.VMEM((layers, outer, q_seg, LANES), bf16),
            pltpu.VMEM((layers, q_seg, LANES), bf16),
            pltpu.VMEM((layers, q_seg // 2, LANES), bf16),
            dma((phases, parts)),
            dma((phases, parts)),
            dma((phases, parts)),
            dma((phases, parts)),
            dma((3,)),
            dma((3,)),
            dma((layers, 4, outer + 1)),
            dma((layers, 4, outer + 1)),
        ],
        compiler_params=pltpu.CompilerParams(
            collective_id=0, has_side_effects=True, vmem_limit_bytes=60 * 1024 * 1024
        ),
        cost_estimate=pl.CostEstimate(
            flops=14 * 10**9, bytes_accessed=12 * 10**6, transcendentals=rows * units * 4
        ),
    )(
        inverse,
        cell_count,
        listed,
        feats,
        tile_val,
        out_grad,
        gate_weight_matrix,
        w_up,
        w_down,
    )


def solution(mesh):
    return jax.shard_map(
        functools.partial(local, mesh.shape["dom"]),
        mesh=mesh,
        in_specs=(
            P(("groups", "dom"), None),
            P(("groups", "dom")),
            P(("groups", "dom"), None),
            P(("groups", "dom"), None, None, None),
            P(("groups", "dom"), None, None),
            P(("groups", "dom"), None),
            P(("groups", "dom"), None, None),
            P(None, None, "mp"),
            P(None, None, "mp"),
            P(None, "mp", None),
            P(("groups", "dom"), None),
        ),
        out_specs=(
            P(("groups", "dom"), None),
            P(("groups", "dom"), None),
            P("groups", None, "mp"),
            P("groups", None, "mp"),
            P("groups", "mp", None),
        ),
        check_vma=False,
    )
```

```python
import functools

import jax
import jax.numpy as jnp
from jax import lax
from jax.experimental import pallas as pl
from jax.experimental.pallas import tpu as pltpu
from jax.sharding import PartitionSpec as P

MESH = pl.DeviceIdType.MESH
BLOCK = 128
LANES = 128
TILE = 256


def dot_nn(left, right):
    return lax.dot_general(
        left, right, (((1,), (0,)), ((), ())), preferred_element_type=jnp.float32
    )


def dot_nt(left, right):
    return lax.dot_general(
        left, right, (((1,), (1,)), ((), ())), preferred_element_type=jnp.float32
    )


def dot_tn(left, right):
    return lax.dot_general(
        left, right, (((0,), (0,)), ((), ())), preferred_element_type=jnp.float32
    )


def remote(src, dst, send_sem, recv_sem, dom, core):
    return pltpu.make_async_remote_copy(
        src_ref=src,
        dst_ref=dst,
        send_sem=send_sem,
        recv_sem=recv_sem,
        device_id={"dom": dom, "mp": core},
        device_id_type=MESH,
    )


def aligned(index, size):
    if isinstance(index, int):
        return pl.ds(index * size, size)
    return pl.ds(pl.multiple_of(index * size, size), size)


def kernel(
    parts,
    inv_ref,
    count_ref,
    idx_ref,
    feats_ref,
    tiles_ref,
    cot_ref,
    wg_in,
    wu_in,
    wd_in,
    final_ref,
    fg_ref,
    gg_out,
    gu_out,
    gd_out,
    adj,
    adj_t,
    own_pick,
    s_t,
    r_t,
    states,
    acts,
    hid,
    pre_g,
    pre_u,
    wg,
    wu,
    wd,
    sbuf,
    halo,
    grads,
    res,
    p_one,
    p_sum,
    p_two,
    q_one,
    q_sum,
    q_two,
    h_send,
    h_recv,
    f_send,
    f_recv,
    w_send,
    w_recv,
    a_send,
    a_recv,
):
    me = lax.axis_index("dom")
    core = lax.axis_index("mp")
    sib = 1 - core
    layers = wg_in.shape[0]
    width = feats_ref.shape[1]
    units = wg_in.shape[2]
    rows = feats_ref.shape[0]
    blocks = rows // BLOCK
    tiles = rows // TILE
    slots = sbuf.shape[2]
    outer = parts // 2
    y = lax.rem(me, 2)
    z = me // 2
    f32, bf16 = jnp.float32, jnp.bfloat16

    def each_tile(body):
        for i in range(tiles):
            body(i, 0)

    barrier = pltpu.get_barrier_semaphore()

    def greet(i, _):
        q = lax.rem(me + i, parts)
        pl.semaphore_signal(
            barrier, inc=1, device_id={"dom": q, "mp": core}, device_id_type=MESH
        )
        return 0

    lax.fori_loop(1, parts, greet, 0)
    pl.semaphore_signal(barrier, inc=1, device_id={"dom": me, "mp": sib}, device_id_type=MESH)

    count = count_ref[0]

    def mask_of(i):
        index = lax.broadcasted_iota(jnp.int32, (TILE, 1), 0) + i * TILE
        return (index < count).astype(f32)

    def mask_rows(i, _):
        at = aligned(i, TILE)
        states[0, at, :] = (feats_ref[at, :].astype(f32) * mask_of(i)).astype(bf16)
        return 0

    each_tile(mask_rows)

    columns = jnp.transpose(idx_ref[...])
    own_rows = parts * slots
    own_cols = jnp.where(core == 0, columns[:own_rows], columns[own_rows:])
    step = min(own_rows, TILE)
    for begin in range(0, own_rows, step):
        lane = lax.broadcasted_iota(jnp.int32, (step, rows), 1)
        own_pick[begin : begin + step, :] = (own_cols[begin : begin + step, 0:1] == lane).astype(
            f32
        ).astype(bf16)

    pl.semaphore_wait(barrier, parts)

    def halo_send(phase, onehot, source):
        for begin in range(0, own_rows, step):
            picked = dot_nn(onehot[begin : begin + step, :], source[...]).astype(bf16)
            sbuf[phase, begin // slots : (begin + step) // slots] = picked.reshape(
                step // slots, slots, width
            )
        halo[phase, core, me] = sbuf[phase, me]

        def send(i, _):
            q = lax.rem(me + i, parts)
            remote(
                sbuf.at[phase, q],
                halo.at[phase, core, me],
                h_send.at[phase, q],
                h_recv.at[phase, me],
                q,
                core,
            ).start()
            return 0

        lax.fori_loop(1, parts, send, 0)
        forward(phase, me).start()

    def forward(phase, s):
        return remote(
            halo.at[phase, core, s],
            halo.at[phase, core, s],
            f_send.at[phase, s],
            f_recv.at[phase, s],
            me,
            sib,
        )

    def arrival(phase, s):
        return remote(
            sbuf.at[phase, s],
            halo.at[phase, core, s],
            h_send.at[phase, s],
            h_recv.at[phase, s],
            s,
            core,
        )

    def halo_recv(phase):
        def take(i, _):
            s = lax.rem(me + parts - i, parts)
            arrival(phase, s).wait_recv()
            forward(phase, s).start()
            return 0

        lax.fori_loop(1, parts, take, 0)

        def settle(s, _):
            remote(
                halo.at[phase, sib, s],
                halo.at[phase, sib, s],
                f_send.at[phase, s],
                f_recv.at[phase, s],
                me,
                sib,
            ).wait_recv()
            return 0

        lax.fori_loop(0, parts, settle, 0)

    def landed_rows(phase):
        return halo[phase].reshape(2 * own_rows, width)

    halo_send(0, own_pick, states.at[0])

    weight_copies = []
    for k, (src, dst) in enumerate(((wg_in, wg), (wu_in, wu), (wd_in, wd))):
        copy = remote(src, dst.at[core], w_send.at[k], w_recv.at[k], me, sib)
        copy.start()
        weight_copies.append(copy)
        dst[core] = src[...]

    def build(r, _):
        for c in range(blocks):
            j = inv_ref[r, c]
            tile = tiles_ref[r, jnp.maximum(j, 0)]
            adj[aligned(r, BLOCK), c * BLOCK : (c + 1) * BLOCK] = jnp.where(
                j >= 0, tile, jnp.zeros_like(tile)
            )
        return 0

    lax.fori_loop(0, blocks, build, 0)

    def build_send(i, _):
        at = aligned(i, TILE)
        index = lax.broadcasted_iota(jnp.int32, (TILE, 2 * own_rows), 0) + i * TILE
        s_t[at, :] = (idx_ref[0:1, :] == index).astype(f32).astype(bf16)
        return 0

    def build_receive(i, _):
        at = aligned(i, TILE)
        index = lax.broadcasted_iota(jnp.int32, (TILE, 2 * own_rows), 0) + i * TILE
        r_t[at, :] = (idx_ref[1:2, :] == index).astype(f32).astype(bf16)
        return 0

    def build_back():
        for begin in range(0, own_rows, step):
            lane = lax.broadcasted_iota(jnp.int32, (step, rows), 1)
            own_pick[begin : begin + step, :] = (own_cols[begin : begin + step, 1:2] == lane).astype(
                f32
            ).astype(bf16)

    def turn_tiles():
        def turn(r, _):
            for c in range(blocks):
                adj_t[c * BLOCK : (c + 1) * BLOCK, aligned(r, BLOCK)] = jnp.transpose(
                    adj[aligned(r, BLOCK), c * BLOCK : (c + 1) * BLOCK]
                )
            return 0

        lax.fori_loop(0, blocks, turn, 0)

    for layer in range(layers):
        if layer:
            halo_send(layer, own_pick, states.at[layer])
        state = states.at[layer]

        for begin in range(0, rows, 2 * TILE):
            at = pl.ds(begin, 2 * TILE)
            fg_ref[at, :] = dot_nn(adj[at, :], state[...])
        if layer == 0:
            each_tile(build_receive)
            for copy in weight_copies:
                copy.wait_recv()
        if layer == layers - 1:
            build_back()
            each_tile(build_send)
            turn_tiles()
        halo_recv(layer)

        def mlp(i, _, layer=layer, state=state):
            at = aligned(i, TILE)
            act = (fg_ref[at, :] + dot_nn(r_t[at, :], landed_rows(layer))).astype(bf16)
            acts[layer, at, :] = act
            mixed = jnp.zeros((TILE, width), f32)
            for h in range(2):
                gate = dot_nn(act, wg[h, layer])
                up = dot_nn(act, wu[h, layer])
                sg = 0.5 * jnp.tanh(0.5 * gate) + 0.5
                silu = gate * sg
                hidden = (silu * up).astype(bf16)
                hid[layer, h, at, :] = hidden
                pre_g[layer, h, at, :] = (up * (sg * (1.0 + gate * (1.0 - sg)))).astype(bf16)
                pre_u[layer, h, at, :] = silu.astype(bf16)
                mixed = mixed + dot_nn(hidden, wd[h, layer])
            new = ((state[at, :].astype(f32) + mixed) * mask_of(i)).astype(bf16)
            if layer + 1 < layers:
                states[layer + 1, at, :] = new
            else:
                final_ref[at, :] = new
            return 0

        each_tile(mlp)

    total = grads.shape[1]
    p_rows = total * 2 // 3
    p_half = p_rows // 2
    p_seg = p_half // outer
    q_seg = (total - p_rows) // outer
    q_half = q_seg // 2

    def at_rows(base, index, size):
        return pl.ds(pl.multiple_of(base + index * size, 16), size)

    def each_other(fn):
        def go(i, _):
            fn(lax.rem(z + i, outer))
            return 0

        lax.fori_loop(1, outer, go, 0)

    def pair(stage, layer, src, dst):
        return remote(
            src,
            dst,
            a_send.at[layer, stage, outer],
            a_recv.at[layer, stage, outer],
            z * 2 + 1 - y,
            core,
        )

    def line(stage, layer, src, dst, to, slot):
        return remote(
            src,
            dst,
            a_send.at[layer, stage, to],
            a_recv.at[layer, stage, slot],
            to * 2 + y,
            core,
        )

    def reduce_one(layer):
        pair(0, layer, grads.at[layer, at_rows(0, 1 - y, p_half)], p_one.at[layer]).start()
        each_other(
            lambda t: line(
                0,
                layer,
                grads.at[layer, at_rows(p_rows, t, q_seg)],
                q_one.at[layer, z],
                t,
                z,
            ).start()
        )
        q_one[layer, z] = grads[layer, at_rows(p_rows, z, q_seg)]

    def reduce_two(layer):
        pair(0, layer, grads.at[layer, at_rows(0, 1 - y, p_half)], p_one.at[layer]).wait_recv()
        p_sum[layer] = (
            grads[layer, at_rows(0, y, p_half)].astype(f32) + p_one[layer].astype(f32)
        ).astype(bf16)
        each_other(
            lambda t: line(
                1, layer, p_sum.at[layer, at_rows(0, t, p_seg)], p_two.at[layer, z], t, z
            ).start()
        )
        p_two[layer, z] = p_sum[layer, at_rows(0, z, p_seg)]
        each_other(
            lambda t: line(
                0,
                layer,
                grads.at[layer, at_rows(p_rows, t, q_seg)],
                q_one.at[layer, t],
                t,
                t,
            ).wait_recv()
        )
        q_sum[layer] = jnp.sum(q_one[layer].astype(f32), axis=0).astype(bf16)
        pair(1, layer, q_sum.at[layer, at_rows(0, 1 - y, q_half)], q_two.at[layer]).start()

    def reduce_three(layer):
        each_other(
            lambda t: line(
                1, layer, p_sum.at[layer, at_rows(0, t, p_seg)], p_two.at[layer, t], t, t
            ).wait_recv()
        )
        mine = at_rows(y * p_half, z, p_seg)
        res[layer, mine] = jnp.sum(p_two[layer].astype(f32), axis=0).astype(bf16)
        each_other(
            lambda t: line(2, layer, res.at[layer, mine], res.at[layer, mine], t, z).start()
        )
        pair(1, layer, q_sum.at[layer, at_rows(0, 1 - y, q_half)], q_two.at[layer]).wait_recv()
        own = at_rows(p_rows + z * q_seg, y, q_half)
        res[layer, own] = (
            q_sum[layer, at_rows(0, y, q_half)].astype(f32) + q_two[layer].astype(f32)
        ).astype(bf16)
        pair(2, layer, res.at[layer, own], res.at[layer, own]).start()

    def reduce_four(layer):
        def landed(t):
            there = at_rows(y * p_half, t, p_seg)
            line(2, layer, res.at[layer, there], res.at[layer, there], t, t).wait_recv()

        each_other(landed)
        half = at_rows(0, y, p_half)
        pair(3, layer, res.at[layer, half], res.at[layer, half]).start()
        other = at_rows(p_rows + z * q_seg, 1 - y, q_half)
        pair(2, layer, res.at[layer, other], res.at[layer, other]).wait_recv()
        own = at_rows(p_rows, z, q_seg)
        each_other(lambda t: line(3, layer, res.at[layer, own], res.at[layer, own], t, z).start())

    def reduce_end(layer):
        half = at_rows(0, 1 - y, p_half)
        pair(3, layer, res.at[layer, half], res.at[layer, half]).wait_recv()

        def landed(t):
            there = at_rows(p_rows, t, q_seg)
            line(3, layer, res.at[layer, there], res.at[layer, there], t, t).wait_recv()

        each_other(landed)
        at = 0
        for out in (gg_out, gu_out, gd_out):
            height, wide = out.shape[1:]
            for c in range(0, wide, LANES):
                out[layer, :, c : c + LANES] = res[layer, at : at + height].astype(f32)
                at += height

    def reduce_drain(layer):
        pair(0, layer, grads.at[layer, at_rows(0, 1 - y, p_half)], p_one.at[layer]).wait_send()
        pair(1, layer, q_sum.at[layer, at_rows(0, 1 - y, q_half)], q_two.at[layer]).wait_send()
        own = at_rows(p_rows + z * q_seg, y, q_half)
        pair(2, layer, res.at[layer, own], res.at[layer, own]).wait_send()
        half = at_rows(0, y, p_half)
        pair(3, layer, res.at[layer, half], res.at[layer, half]).wait_send()
        mine = at_rows(y * p_half, z, p_seg)
        whole = at_rows(p_rows, z, q_seg)

        def sent(t):
            line(
                0,
                layer,
                grads.at[layer, at_rows(p_rows, t, q_seg)],
                q_one.at[layer, z],
                t,
                z,
            ).wait_send()
            line(
                1, layer, p_sum.at[layer, at_rows(0, t, p_seg)], p_two.at[layer, z], t, z
            ).wait_send()
            line(2, layer, res.at[layer, mine], res.at[layer, mine], t, z).wait_send()
            line(3, layer, res.at[layer, whole], res.at[layer, whole], t, z).wait_send()

        each_other(sent)

    down_in, agg_grad = states.at[0], states.at[1]

    def start_rows(i, _):
        at = aligned(i, TILE)
        fg_ref[at, :] = cot_ref[at, :].astype(f32) * mask_of(i)
        return 0

    each_tile(start_rows)

    for layer in reversed(range(layers)):
        phase = 2 * layers - 1 - layer
        last = layer == layers - 1

        def mlp_back(i, _, layer=layer):
            at = aligned(i, TILE)
            down = fg_ref[at, :].astype(bf16)
            down_in[at, :] = down
            for h in range(2):
                hidden_grad = dot_nt(down, wd[h, layer])
                gate_grad = (hidden_grad * pre_g[layer, h, at, :].astype(f32)).astype(bf16)
                up_grad = (hidden_grad * pre_u[layer, h, at, :].astype(f32)).astype(bf16)
                pre_g[layer, h, at, :] = gate_grad
                pre_u[layer, h, at, :] = up_grad
            return 0

        def through_weights(i, _, layer=layer):
            at = aligned(i, TILE)
            total = jnp.zeros((TILE, width), f32)
            for h in range(2):
                total = total + dot_nt(pre_g[layer, h, at, :], wg[h, layer])
                total = total + dot_nt(pre_u[layer, h, at, :], wu[h, layer])
            agg_grad[at, :] = total.astype(bf16)
            return 0

        def weight_gradients(layer=layer):
            at = 0
            act = acts[layer]
            for left, right in (
                (act, pre_g[layer, core]),
                (act, pre_u[layer, core]),
                (hid[layer, core], down_in[...]),
            ):
                part = dot_tn(left, right).astype(bf16)
                for c in range(0, part.shape[1], LANES):
                    grads[layer, at : at + part.shape[0], :] = part[:, c : c + LANES]
                    at += part.shape[0]
            reduce_one(layer)

        each_tile(mlp_back)
        if layer == 0:
            if not last:
                reduce_three(layer + 1)
            weight_gradients()
        each_tile(through_weights)
        halo_send(phase, own_pick, agg_grad)
        if layer:
            if not last:
                reduce_three(layer + 1)
            weight_gradients()
        if not last:
            reduce_four(layer + 1)

        for begin in range(0, rows, 2 * TILE):
            at = pl.ds(begin, 2 * TILE)
            fg_ref[at, :] = fg_ref[at, :] + dot_nn(adj_t[at, :], agg_grad[...])
        if not last:
            reduce_two(layer)
        halo_recv(phase)

        def finish(i, _, phase=phase):
            at = aligned(i, TILE)
            fg_ref[at, :] = (fg_ref[at, :] + dot_nn(s_t[at, :], landed_rows(phase))) * mask_of(i)
            return 0

        each_tile(finish)
        if last:
            reduce_two(layer)
        else:
            reduce_end(layer + 1)

    reduce_three(0)
    reduce_four(0)
    reduce_end(0)
    for layer in range(layers):
        reduce_drain(layer)
    for copy in weight_copies:
        copy.wait_send()
    for phase in range(2 * layers):

        def drained(i, _, phase=phase):
            q = lax.rem(me + i, parts)
            arrival(phase, q).wait_send()
            forward(phase, q).wait_send()
            return 0

        lax.fori_loop(1, parts, drained, 0)
        forward(phase, me).wait_send()


def hand_over(*refs):
    sems = refs[-1]
    count = (len(refs) - 1) // 2
    copies = []
    for k in range(count):
        source, target = refs[k], refs[count + k]
        cuts = 2 if source.shape[0] < 8 else 4
        size = source.shape[0] // cuts
        for cut in range(cuts):
            at = pl.ds(cut * size, size)
            copies.append(
                pltpu.make_async_copy(source.at[at], target.at[at], sems.at[k, cut])
            )
    for copy in copies:
        copy.start()
    for copy in copies:
        copy.wait()


def local(
    parts,
    feats,
    cell_count,
    tile_col,
    tile_val,
    send_list,
    send_count,
    recv_list,
    gate_weight_matrix,
    w_up,
    w_down,
    out_grad,
):
    rows, width = feats.shape
    layers, _, units = gate_weight_matrix.shape
    blocks, per_row = tile_col.shape
    slot_count = send_list.shape[2]
    half = slot_count // 2
    outer = parts // 2
    all_slots = parts * slot_count
    position = jnp.arange(1, per_row + 1, dtype=jnp.int32)[None, :, None]
    chosen = tile_col[:, :, None] == jnp.arange(blocks, dtype=jnp.int32)[None, None, :]
    inverse = jnp.sum(jnp.where(chosen, position, 0), axis=1) - 1
    live = jnp.arange(slot_count)[None, :] < send_count[0][:, None]
    listed = jnp.stack([jnp.where(live, send_list[0], -1), recv_list[0]])
    listed = jnp.swapaxes(listed.reshape(2, parts, 2, half), 1, 2).reshape(2, all_slots)
    listed = jnp.pad(listed, ((0, 6), (0, 0)))

    total = 2 * width * (units // LANES) + units * (width // LANES)
    p_half = total // 3
    q_seg = (total - 2 * p_half) // outer
    f32, bf16 = jnp.float32, jnp.bfloat16
    vmem = pl.BlockSpec(memory_space=pltpu.VMEM)
    smem = pl.BlockSpec(memory_space=pltpu.SMEM)
    phases = 2 * layers
    dma = pltpu.SemaphoreType.DMA
    outs = pl.pallas_call(
        functools.partial(kernel, parts),
        out_shape=(
            jax.ShapeDtypeStruct((rows, width), bf16),
            jax.ShapeDtypeStruct((rows, width), f32),
            jax.ShapeDtypeStruct((layers, width, units), f32),
            jax.ShapeDtypeStruct((layers, width, units), f32),
            jax.ShapeDtypeStruct((layers, units, width), f32),
        ),
        in_specs=[smem, smem] + [vmem] * 7,
        out_specs=[vmem] * 5,
        scratch_shapes=[
            pltpu.VMEM((rows, rows), bf16),
            pltpu.VMEM((rows, rows), bf16),
            pltpu.VMEM((all_slots // 2, rows), bf16),
            pltpu.VMEM((rows, all_slots), bf16),
            pltpu.VMEM((rows, all_slots), bf16),
            pltpu.VMEM((max(layers, 2), rows, width), bf16),
            pltpu.VMEM((layers, rows, width), bf16),
            pltpu.VMEM((layers, 2, rows, units), bf16),
            pltpu.VMEM((layers, 2, rows, units), bf16),
            pltpu.VMEM((layers, 2, rows, units), bf16),
            pltpu.VMEM((2, layers, width, units), bf16),
            pltpu.VMEM((2, layers, width, units), bf16),
            pltpu.VMEM((2, layers, units, width), bf16),
            pltpu.VMEM((phases, parts, half, width), bf16),
            pltpu.VMEM((phases, 2, parts, half, width), bf16),
            pltpu.VMEM((layers, total, LANES), bf16),
            pltpu.VMEM((layers, total, LANES), bf16),
            pltpu.VMEM((layers, p_half, LANES), bf16),
            pltpu.VMEM((layers, p_half, LANES), bf16),
            pltpu.VMEM((layers, outer, p_half // outer, LANES), bf16),
            pltpu.VMEM((layers, outer, q_seg, LANES), bf16),
            pltpu.VMEM((layers, q_seg, LANES), bf16),
            pltpu.VMEM((layers, q_seg // 2, LANES), bf16),
            dma((phases, parts)),
            dma((phases, parts)),
            dma((phases, parts)),
            dma((phases, parts)),
            dma((3,)),
            dma((3,)),
            dma((layers, 4, outer + 1)),
            dma((layers, 4, outer + 1)),
        ],
        compiler_params=pltpu.CompilerParams(
            collective_id=0, has_side_effects=True, vmem_limit_bytes=60 * 1024 * 1024
        ),
        cost_estimate=pl.CostEstimate(
            flops=14 * 10**9, bytes_accessed=12 * 10**6, transcendentals=rows * units * 4
        ),
    )(
        inverse,
        cell_count,
        listed,
        feats,
        tile_val,
        out_grad,
        gate_weight_matrix,
        w_up,
        w_down,
    )
    return pl.pallas_call(
        hand_over,
        out_shape=tuple(jax.ShapeDtypeStruct(out.shape, out.dtype) for out in outs),
        in_specs=[pl.BlockSpec(memory_space=pl.ANY)] * len(outs),
        out_specs=[pl.BlockSpec(memory_space=pl.ANY)] * len(outs),
        scratch_shapes=[dma((len(outs), 4))],
    )(*outs)


def solution(mesh):
    return jax.shard_map(
        functools.partial(local, mesh.shape["dom"]),
        mesh=mesh,
        in_specs=(
            P(("groups", "dom"), None),
            P(("groups", "dom")),
            P(("groups", "dom"), None),
            P(("groups", "dom"), None, None, None),
            P(("groups", "dom"), None, None),
            P(("groups", "dom"), None),
            P(("groups", "dom"), None, None),
            P(None, None, "mp"),
            P(None, None, "mp"),
            P(None, "mp", None),
            P(("groups", "dom"), None),
        ),
        out_specs=(
            P(("groups", "dom"), None),
            P(("groups", "dom"), None),
            P("groups", None, "mp"),
            P("groups", None, "mp"),
            P("groups", "mp", None),
        ),
        check_vma=False,
    )
```

```python
import functools

import jax
import jax.numpy as jnp
from jax import lax
from jax.experimental import pallas as pl
from jax.experimental.pallas import tpu as pltpu
from jax.sharding import PartitionSpec as P

MESH = pl.DeviceIdType.MESH
BLOCK = 128
LANES = 128
TILE = 256


def dot_nn(left, right):
    return lax.dot_general(
        left, right, (((1,), (0,)), ((), ())), preferred_element_type=jnp.float32
    )


def remote(src, dst, send_sem, recv_sem, dom, core):
    return pltpu.make_async_remote_copy(
        src_ref=src,
        dst_ref=dst,
        send_sem=send_sem,
        recv_sem=recv_sem,
        device_id={"dom": dom, "mp": core},
        device_id_type=MESH,
    )


def aligned(index, size):
    if isinstance(index, int):
        return pl.ds(index * size, size)
    return pl.ds(pl.multiple_of(index * size, size), size)


def kernel(
    parts,
    col_ref,
    count_ref,
    send_ref,
    live_ref,
    recv_ref,
    feats_ref,
    tiles_in,
    cot_in,
    wg_in,
    wu_in,
    wd_in,
    final_out,
    fg_out,
    gg_out,
    gu_out,
    gd_out,
    idx_ref,
    tiles_ref,
    cot_ref,
    final_ref,
    fg_ref,
    gg_ref,
    gu_ref,
    gd_ref,
    adj,
    adj_t,
    own_pick,
    s_t,
    r_t,
    states,
    acts_t,
    hid_t,
    pre_g,
    pre_u,
    wg,
    wu,
    wd,
    wg_t,
    wu_t,
    wd_t,
    sbuf,
    halo,
    grads,
    res,
    p_one,
    p_sum,
    p_two,
    q_one,
    q_sum,
    q_two,
    h_send,
    h_recv,
    f_send,
    f_recv,
    w_send,
    w_recv,
    a_send,
    a_recv,
    i_sem,
    o_sem,
):
    me = lax.axis_index("dom")
    core = lax.axis_index("mp")
    sib = 1 - core
    layers = wg_in.shape[0]
    width = feats_ref.shape[1]
    units = wg_in.shape[2]
    rows = feats_ref.shape[0]
    blocks = rows // BLOCK
    tiles = rows // TILE
    slots = sbuf.shape[2]
    outer = parts // 2
    y = lax.rem(me, 2)
    z = me // 2
    f32, bf16 = jnp.float32, jnp.bfloat16

    def each_tile(body):
        for i in range(tiles):
            body(i, 0)

    barrier = pltpu.get_barrier_semaphore()

    def greet(i, _):
        q = lax.rem(me + i, parts)
        pl.semaphore_signal(
            barrier, inc=1, device_id={"dom": q, "mp": core}, device_id_type=MESH
        )
        return 0

    load_tiles = pltpu.make_async_copy(tiles_in, tiles_ref, i_sem.at[0])
    load_cot = pltpu.make_async_copy(cot_in, cot_ref, i_sem.at[1])
    load_weights = [
        pltpu.make_async_copy(src, dst.at[core], i_sem.at[2 + k])
        for k, (src, dst) in enumerate(((wg_in, wg), (wu_in, wu), (wd_in, wd)))
    ]
    lax.fori_loop(1, parts, greet, 0)
    pl.semaphore_signal(barrier, inc=1, device_id={"dom": me, "mp": sib}, device_id_type=MESH)

    for copy in load_weights:
        copy.start()
    load_tiles.start()
    load_cot.start()
    count = count_ref[0]

    def mask_of(i):
        index = lax.broadcasted_iota(jnp.int32, (TILE, 1), 0) + i * TILE
        return (index < count).astype(f32)

    def mask_rows(i, _):
        at = aligned(i, TILE)
        states[0, at, :] = (feats_ref[at, :].astype(f32) * mask_of(i)).astype(bf16)
        return 0

    each_tile(mask_rows)

    own_rows = parts * slots
    step = min(own_rows, TILE)
    slot = lax.broadcasted_iota(jnp.int32, (2 * slots, parts), 0)
    sources = jnp.where(slot < live_ref[...], jnp.transpose(send_ref[0]), -1)
    targets = jnp.transpose(recv_ref[0])

    def pick_rows(listed):
        for q in range(parts):
            column = listed[:, q : q + 1]
            column = jnp.where(core == 0, column[:slots], column[slots:])
            lane = lax.broadcasted_iota(jnp.int32, (slots, rows), 1)
            own_pick[q * slots : (q + 1) * slots, :] = (column == lane).astype(f32).astype(bf16)

    def lay_out(place, listed):
        pieces = [
            listed[h * slots : (h + 1) * slots, q : q + 1]
            for h in range(2)
            for q in range(parts)
        ]
        per = LANES // slots
        for k in range(0, len(pieces), per):
            column = jnp.concatenate(pieces[k : k + per], axis=0)
            across = jnp.transpose(jnp.broadcast_to(column, (LANES, LANES)))
            idx_ref[place : place + 1, k * slots : k * slots + LANES] = across[0:1, :]

    pick_rows(sources)
    pl.semaphore_wait(barrier, parts)

    def halo_send(phase, onehot, source):
        for begin in range(0, own_rows, step):
            picked = dot_nn(onehot[begin : begin + step, :], source[...]).astype(bf16)
            sbuf[phase, begin // slots : (begin + step) // slots] = picked.reshape(
                step // slots, slots, width
            )
        halo[phase, core, me] = sbuf[phase, me]

        def send(i, _):
            q = lax.rem(me + i, parts)
            remote(
                sbuf.at[phase, q],
                halo.at[phase, core, me],
                h_send.at[phase, q],
                h_recv.at[phase, me],
                q,
                core,
            ).start()
            return 0

        lax.fori_loop(1, parts, send, 0)
        forward(phase, me).start()

    def forward(phase, s):
        return remote(
            halo.at[phase, core, s],
            halo.at[phase, core, s],
            f_send.at[phase, s],
            f_recv.at[phase, s],
            me,
            sib,
        )

    def arrival(phase, s):
        return remote(
            sbuf.at[phase, s],
            halo.at[phase, core, s],
            h_send.at[phase, s],
            h_recv.at[phase, s],
            s,
            core,
        )

    def halo_recv(phase):
        def take(i, _):
            s = lax.rem(me + parts - i, parts)
            arrival(phase, s).wait_recv()
            forward(phase, s).start()
            return 0

        lax.fori_loop(1, parts, take, 0)

        def settle(s, _):
            remote(
                halo.at[phase, sib, s],
                halo.at[phase, sib, s],
                f_send.at[phase, s],
                f_recv.at[phase, s],
                me,
                sib,
            ).wait_recv()
            return 0

        lax.fori_loop(0, parts, settle, 0)

    def landed_rows(phase):
        return halo[phase].reshape(2 * own_rows, width)

    halo_send(0, own_pick, states.at[0])

    weight_copies = []
    for k, (src, dst) in enumerate(((wg_in, wg), (wu_in, wu), (wd_in, wd))):
        load_weights[k].wait()
        copy = remote(dst.at[core], dst.at[core], w_send.at[k], w_recv.at[k], me, sib)
        copy.start()
        weight_copies.append(copy)

    load_tiles.wait()
    lay_out(1, targets)

    def build(r, _):
        held = [col_ref[r, j] for j in range(tiles_ref.shape[1])]
        for c in range(blocks):
            j = jnp.int32(-1)
            for k, col in enumerate(held):
                j = jnp.where(col == c, k, j)
            tile = tiles_ref[r, jnp.maximum(j, 0)]
            adj[aligned(r, BLOCK), c * BLOCK : (c + 1) * BLOCK] = jnp.where(
                j >= 0, tile, jnp.zeros_like(tile)
            )
        return 0

    lax.fori_loop(0, blocks, build, 0)

    def build_send(i, _):
        at = aligned(i, TILE)
        index = lax.broadcasted_iota(jnp.int32, (TILE, 2 * own_rows), 0) + i * TILE
        s_t[at, :] = (idx_ref[0:1, :] == index).astype(f32).astype(bf16)
        return 0

    def build_receive(i, _):
        at = aligned(i, TILE)
        index = lax.broadcasted_iota(jnp.int32, (TILE, 2 * own_rows), 0) + i * TILE
        r_t[at, :] = (idx_ref[1:2, :] == index).astype(f32).astype(bf16)
        return 0

    def turn_tiles():
        def turn(r, _):
            for c in range(blocks):
                adj_t[c * BLOCK : (c + 1) * BLOCK, aligned(r, BLOCK)] = jnp.transpose(
                    adj[aligned(r, BLOCK), c * BLOCK : (c + 1) * BLOCK]
                )
            return 0

        lax.fori_loop(0, blocks, turn, 0)

    for layer in range(layers):
        if layer:
            halo_send(layer, own_pick, states.at[layer])
        state = states.at[layer]

        for begin in range(0, rows, 2 * TILE):
            at = pl.ds(begin, 2 * TILE)
            fg_ref[at, :] = dot_nn(adj[at, :], state[...])
        if layer == 0:
            each_tile(build_receive)
            for copy in weight_copies:
                copy.wait_recv()
        if layer == layers - 1:
            pick_rows(targets)
            lay_out(0, sources)
            each_tile(build_send)
            turn_tiles()
            for plain, turned in ((wg, wg_t), (wu, wu_t), (wd, wd_t)):
                for h in range(2):
                    for k in range(layers):
                        turned[h, k] = jnp.transpose(plain[h, k])
        halo_recv(layer)

        def mlp(i, _, layer=layer, state=state):
            at = aligned(i, TILE)
            act = (fg_ref[at, :] + dot_nn(r_t[at, :], landed_rows(layer))).astype(bf16)
            acts_t[layer, :, at] = jnp.transpose(act)
            made = []
            mixed = jnp.zeros((TILE, width), f32)
            for h in range(2):
                gate = dot_nn(act, wg[h, layer])
                up = dot_nn(act, wu[h, layer])
                sg = 0.5 * jnp.tanh(0.5 * gate) + 0.5
                silu = gate * sg
                hidden = (silu * up).astype(bf16)
                made.append(hidden)
                pre_g[layer, h, at, :] = (up * (sg * (1.0 + gate * (1.0 - sg)))).astype(bf16)
                pre_u[layer, h, at, :] = silu.astype(bf16)
                mixed = mixed + dot_nn(hidden, wd[h, layer])
            hid_t[layer, :, at] = jnp.transpose(jnp.where(core == 0, made[0], made[1]))
            new = ((state[at, :].astype(f32) + mixed) * mask_of(i)).astype(bf16)
            if layer + 1 < layers:
                states[layer + 1, at, :] = new
            else:
                final_ref[at, :] = new
            return 0

        each_tile(mlp)

    total = grads.shape[1]
    p_rows = total * 2 // 3
    p_half = p_rows // 2
    p_seg = p_half // outer
    q_seg = (total - p_rows) // outer
    q_half = q_seg // 2

    def at_rows(base, index, size):
        return pl.ds(pl.multiple_of(base + index * size, 16), size)

    def each_other(fn):
        def go(i, _):
            fn(lax.rem(z + i, outer))
            return 0

        lax.fori_loop(1, outer, go, 0)

    def pair(stage, layer, src, dst):
        return remote(
            src,
            dst,
            a_send.at[layer, stage, outer],
            a_recv.at[layer, stage, outer],
            z * 2 + 1 - y,
            core,
        )

    def line(stage, layer, src, dst, to, slot):
        return remote(
            src,
            dst,
            a_send.at[layer, stage, to],
            a_recv.at[layer, stage, slot],
            to * 2 + y,
            core,
        )

    def reduce_one(layer):
        pair(0, layer, grads.at[layer, at_rows(0, 1 - y, p_half)], p_one.at[layer]).start()
        each_other(
            lambda t: line(
                0,
                layer,
                grads.at[layer, at_rows(p_rows, t, q_seg)],
                q_one.at[layer, z],
                t,
                z,
            ).start()
        )
        q_one[layer, z] = grads[layer, at_rows(p_rows, z, q_seg)]

    def reduce_two(layer):
        pair(0, layer, grads.at[layer, at_rows(0, 1 - y, p_half)], p_one.at[layer]).wait_recv()
        p_sum[layer] = (
            grads[layer, at_rows(0, y, p_half)].astype(f32) + p_one[layer].astype(f32)
        ).astype(bf16)
        each_other(
            lambda t: line(
                1, layer, p_sum.at[layer, at_rows(0, t, p_seg)], p_two.at[layer, z], t, z
            ).start()
        )
        p_two[layer, z] = p_sum[layer, at_rows(0, z, p_seg)]
        each_other(
            lambda t: line(
                0,
                layer,
                grads.at[layer, at_rows(p_rows, t, q_seg)],
                q_one.at[layer, t],
                t,
                t,
            ).wait_recv()
        )
        q_sum[layer] = jnp.sum(q_one[layer].astype(f32), axis=0).astype(bf16)
        pair(1, layer, q_sum.at[layer, at_rows(0, 1 - y, q_half)], q_two.at[layer]).start()

    def reduce_three(layer):
        each_other(
            lambda t: line(
                1, layer, p_sum.at[layer, at_rows(0, t, p_seg)], p_two.at[layer, t], t, t
            ).wait_recv()
        )
        mine = at_rows(y * p_half, z, p_seg)
        res[layer, mine] = jnp.sum(p_two[layer].astype(f32), axis=0).astype(bf16)
        each_other(
            lambda t: line(2, layer, res.at[layer, mine], res.at[layer, mine], t, z).start()
        )
        pair(1, layer, q_sum.at[layer, at_rows(0, 1 - y, q_half)], q_two.at[layer]).wait_recv()
        own = at_rows(p_rows + z * q_seg, y, q_half)
        res[layer, own] = (
            q_sum[layer, at_rows(0, y, q_half)].astype(f32) + q_two[layer].astype(f32)
        ).astype(bf16)
        pair(2, layer, res.at[layer, own], res.at[layer, own]).start()

    def reduce_four(layer):
        def landed(t):
            there = at_rows(y * p_half, t, p_seg)
            line(2, layer, res.at[layer, there], res.at[layer, there], t, t).wait_recv()

        each_other(landed)
        half = at_rows(0, y, p_half)
        pair(3, layer, res.at[layer, half], res.at[layer, half]).start()
        other = at_rows(p_rows + z * q_seg, 1 - y, q_half)
        pair(2, layer, res.at[layer, other], res.at[layer, other]).wait_recv()
        own = at_rows(p_rows, z, q_seg)
        each_other(lambda t: line(3, layer, res.at[layer, own], res.at[layer, own], t, z).start())

    def stores(layer):
        return [
            pltpu.make_async_copy(ref.at[layer], out.at[layer], o_sem.at[2 + k, layer])
            for k, (ref, out) in enumerate(((gg_ref, gg_out), (gu_ref, gu_out), (gd_ref, gd_out)))
        ]

    store_final = pltpu.make_async_copy(final_ref, final_out, o_sem.at[0, 0])
    store_final.start()
    store_fg = pltpu.make_async_copy(fg_ref, fg_out, o_sem.at[1, 0])

    def reduce_end(layer):
        half = at_rows(0, 1 - y, p_half)
        pair(3, layer, res.at[layer, half], res.at[layer, half]).wait_recv()

        def landed(t):
            there = at_rows(p_rows, t, q_seg)
            line(3, layer, res.at[layer, there], res.at[layer, there], t, t).wait_recv()

        each_other(landed)
        at = 0
        for out in (gg_ref, gu_ref, gd_ref):
            height, wide = out.shape[1:]
            for c in range(0, wide, LANES):
                out[layer, :, c : c + LANES] = res[layer, at : at + height].astype(f32)
                at += height
        for copy in stores(layer):
            copy.start()

    def reduce_drain(layer):
        pair(0, layer, grads.at[layer, at_rows(0, 1 - y, p_half)], p_one.at[layer]).wait_send()
        pair(1, layer, q_sum.at[layer, at_rows(0, 1 - y, q_half)], q_two.at[layer]).wait_send()
        own = at_rows(p_rows + z * q_seg, y, q_half)
        pair(2, layer, res.at[layer, own], res.at[layer, own]).wait_send()
        half = at_rows(0, y, p_half)
        pair(3, layer, res.at[layer, half], res.at[layer, half]).wait_send()
        mine = at_rows(y * p_half, z, p_seg)
        whole = at_rows(p_rows, z, q_seg)

        def sent(t):
            line(
                0,
                layer,
                grads.at[layer, at_rows(p_rows, t, q_seg)],
                q_one.at[layer, z],
                t,
                z,
            ).wait_send()
            line(
                1, layer, p_sum.at[layer, at_rows(0, t, p_seg)], p_two.at[layer, z], t, z
            ).wait_send()
            line(2, layer, res.at[layer, mine], res.at[layer, mine], t, z).wait_send()
            line(3, layer, res.at[layer, whole], res.at[layer, whole], t, z).wait_send()

        each_other(sent)

    down_in, agg_grad = states.at[0], states.at[1]

    load_cot.wait()

    def start_rows(i, _):
        at = aligned(i, TILE)
        fg_ref[at, :] = cot_ref[at, :].astype(f32) * mask_of(i)
        return 0

    each_tile(start_rows)

    for layer in reversed(range(layers)):
        phase = 2 * layers - 1 - layer
        last = layer == layers - 1

        def mlp_back(i, _, layer=layer):
            at = aligned(i, TILE)
            down = fg_ref[at, :].astype(bf16)
            down_in[at, :] = down
            for h in range(2):
                hidden_grad = dot_nn(down, wd_t[h, layer])
                gate_grad = (hidden_grad * pre_g[layer, h, at, :].astype(f32)).astype(bf16)
                up_grad = (hidden_grad * pre_u[layer, h, at, :].astype(f32)).astype(bf16)
                pre_g[layer, h, at, :] = gate_grad
                pre_u[layer, h, at, :] = up_grad
            return 0

        def through_weights(i, _, layer=layer):
            at = aligned(i, TILE)
            total = jnp.zeros((TILE, width), f32)
            for h in range(2):
                total = total + dot_nn(pre_g[layer, h, at, :], wg_t[h, layer])
                total = total + dot_nn(pre_u[layer, h, at, :], wu_t[h, layer])
            agg_grad[at, :] = total.astype(bf16)
            return 0

        def weight_gradients(layer=layer):
            at = 0
            act = acts_t[layer]
            for left, right in (
                (act, pre_g[layer, core]),
                (act, pre_u[layer, core]),
                (hid_t[layer], down_in[...]),
            ):
                part = dot_nn(left, right).astype(bf16)
                for c in range(0, part.shape[1], LANES):
                    grads[layer, at : at + part.shape[0], :] = part[:, c : c + LANES]
                    at += part.shape[0]
            reduce_one(layer)

        each_tile(mlp_back)
        if layer == 0:
            if not last:
                reduce_three(layer + 1)
            weight_gradients()
        each_tile(through_weights)
        halo_send(phase, own_pick, agg_grad)
        if layer:
            if not last:
                reduce_three(layer + 1)
            weight_gradients()
        if not last:
            reduce_four(layer + 1)

        for begin in range(0, rows, 2 * TILE):
            at = pl.ds(begin, 2 * TILE)
            fg_ref[at, :] = fg_ref[at, :] + dot_nn(adj_t[at, :], agg_grad[...])
        if not last:
            reduce_two(layer)
        halo_recv(phase)

        def finish(i, _, phase=phase):
            at = aligned(i, TILE)
            fg_ref[at, :] = (fg_ref[at, :] + dot_nn(s_t[at, :], landed_rows(phase))) * mask_of(i)
            return 0

        each_tile(finish)
        if last:
            reduce_two(layer)
        else:
            reduce_end(layer + 1)

    store_fg.start()
    reduce_three(0)
    reduce_four(0)
    reduce_end(0)
    store_final.wait()
    store_fg.wait()
    for layer in range(layers):
        reduce_drain(layer)
        for copy in stores(layer):
            copy.wait()
    for copy in weight_copies:
        copy.wait_send()
    for phase in range(2 * layers):

        def drained(i, _, phase=phase):
            q = lax.rem(me + i, parts)
            arrival(phase, q).wait_send()
            forward(phase, q).wait_send()
            return 0

        lax.fori_loop(1, parts, drained, 0)
        forward(phase, me).wait_send()


def hand_over(*refs):
    count = (len(refs) - 2) // 3
    in_sem, out_sem = refs[-2:]
    pairs = []
    for k in range(count):
        source, target, held = refs[k], refs[count + k], refs[2 * count + k]
        cuts = 2 if source.shape[0] < 8 else 4
        size = source.shape[0] // cuts
        for cut in range(cuts):
            at = pl.ds(cut * size, size)
            pairs.append(
                (
                    pltpu.make_async_copy(source.at[at], held.at[at], in_sem.at[k, cut]),
                    pltpu.make_async_copy(held.at[at], target.at[at], out_sem.at[k, cut]),
                )
            )
    for load, _ in pairs:
        load.start()
    for load, store in pairs:
        load.wait()
        store.start()
    for _, store in pairs:
        store.wait()


def local(
    parts,
    feats,
    cell_count,
    tile_col,
    tile_val,
    send_list,
    send_count,
    recv_list,
    gate_weight_matrix,
    w_up,
    w_down,
    out_grad,
):
    rows, width = feats.shape
    layers, _, units = gate_weight_matrix.shape
    slot_count = send_list.shape[2]
    half = slot_count // 2
    outer = parts // 2
    all_slots = parts * slot_count
    total = 2 * width * (units // LANES) + units * (width // LANES)
    p_half = total // 3
    q_seg = (total - 2 * p_half) // outer
    f32, bf16 = jnp.float32, jnp.bfloat16
    vmem = pl.BlockSpec(memory_space=pltpu.VMEM)
    hbm = pl.BlockSpec(memory_space=pl.ANY)
    smem = pl.BlockSpec(memory_space=pltpu.SMEM)
    phases = 2 * layers
    dma = pltpu.SemaphoreType.DMA
    outs = pl.pallas_call(
        functools.partial(kernel, parts),
        out_shape=(
            jax.ShapeDtypeStruct((rows, width), bf16),
            jax.ShapeDtypeStruct((rows, width), f32),
            jax.ShapeDtypeStruct((layers, width, units), f32),
            jax.ShapeDtypeStruct((layers, width, units), f32),
            jax.ShapeDtypeStruct((layers, units, width), f32),
        ),
        in_specs=[smem, smem] + [vmem] * 4 + [hbm] * 5,
        out_specs=[hbm] * 5,
        scratch_shapes=[
            pltpu.VMEM((8, all_slots), jnp.int32),
            pltpu.VMEM(tile_val.shape, bf16),
            pltpu.VMEM((rows, width), bf16),
            pltpu.VMEM((rows, width), bf16),
            pltpu.VMEM((rows, width), f32),
            pltpu.VMEM((layers, width, units), f32),
            pltpu.VMEM((layers, width, units), f32),
            pltpu.VMEM((layers, units, width), f32),
            pltpu.VMEM((rows, rows), bf16),
            pltpu.VMEM((rows, rows), bf16),
            pltpu.VMEM((all_slots // 2, rows), bf16),
            pltpu.VMEM((rows, all_slots), bf16),
            pltpu.VMEM((rows, all_slots), bf16),
            pltpu.VMEM((max(layers, 2), rows, width), bf16),
            pltpu.VMEM((layers, width, rows), bf16),
            pltpu.VMEM((layers, units, rows), bf16),
            pltpu.VMEM((layers, 2, rows, units), bf16),
            pltpu.VMEM((layers, 2, rows, units), bf16),
            pltpu.VMEM((2, layers, width, units), bf16),
            pltpu.VMEM((2, layers, width, units), bf16),
            pltpu.VMEM((2, layers, units, width), bf16),
            pltpu.VMEM((2, layers, units, width), bf16),
            pltpu.VMEM((2, layers, units, width), bf16),
            pltpu.VMEM((2, layers, width, units), bf16),
            pltpu.VMEM((phases, parts, half, width), bf16),
            pltpu.VMEM((phases, 2, parts, half, width), bf16),
            pltpu.VMEM((layers, total, LANES), bf16),
            pltpu.VMEM((layers, total, LANES), bf16),
            pltpu.VMEM((layers, p_half, LANES), bf16),
            pltpu.VMEM((layers, p_half, LANES), bf16),
            pltpu.VMEM((layers, outer, p_half // outer, LANES), bf16),
            pltpu.VMEM((layers, outer, q_seg, LANES), bf16),
            pltpu.VMEM((layers, q_seg, LANES), bf16),
            pltpu.VMEM((layers, q_seg // 2, LANES), bf16),
            dma((phases, parts)),
            dma((phases, parts)),
            dma((phases, parts)),
            dma((phases, parts)),
            dma((3,)),
            dma((3,)),
            dma((layers, 4, outer + 1)),
            dma((layers, 4, outer + 1)),
            dma((5,)),
            dma((5, layers)),
        ],
        compiler_params=pltpu.CompilerParams(
            collective_id=0, has_side_effects=True, vmem_limit_bytes=60 * 1024 * 1024
        ),
        cost_estimate=pl.CostEstimate(
            flops=14 * 10**9, bytes_accessed=12 * 10**6, transcendentals=rows * units * 4
        ),
    )(
        tile_col,
        cell_count,
        send_list,
        send_count,
        recv_list,
        feats,
        tile_val,
        out_grad,
        gate_weight_matrix,
        w_up,
        w_down,
    )
    return pl.pallas_call(
        hand_over,
        out_shape=tuple(jax.ShapeDtypeStruct(out.shape, out.dtype) for out in outs),
        in_specs=[hbm] * len(outs),
        out_specs=[hbm] * len(outs),
        scratch_shapes=[pltpu.VMEM(out.shape, out.dtype) for out in outs]
        + [dma((len(outs), 4)), dma((len(outs), 4))],
        compiler_params=pltpu.CompilerParams(vmem_limit_bytes=60 * 1024 * 1024),
    )(*outs)


def solution(mesh):
    return jax.shard_map(
        functools.partial(local, mesh.shape["dom"]),
        mesh=mesh,
        in_specs=(
            P(("groups", "dom"), None),
            P(("groups", "dom")),
            P(("groups", "dom"), None),
            P(("groups", "dom"), None, None, None),
            P(("groups", "dom"), None, None),
            P(("groups", "dom"), None),
            P(("groups", "dom"), None, None),
            P(None, None, "mp"),
            P(None, None, "mp"),
            P(None, "mp", None),
            P(("groups", "dom"), None),
        ),
        out_specs=(
            P(("groups", "dom"), None),
            P(("groups", "dom"), None),
            P("groups", None, "mp"),
            P("groups", None, "mp"),
            P("groups", "mp", None),
        ),
        check_vma=False,
    )
```

```python
import functools

import jax
import jax.numpy as jnp
from jax import lax
from jax.experimental import pallas as pl
from jax.experimental.pallas import tpu as pltpu
from jax.sharding import PartitionSpec as P

MESH = pl.DeviceIdType.MESH
BLOCK = 128
LANES = 128
TILE = 256


def dot_nn(left, right):
    return lax.dot_general(
        left, right, (((1,), (0,)), ((), ())), preferred_element_type=jnp.float32
    )


def remote(src, dst, send_sem, recv_sem, dom, core):
    return pltpu.make_async_remote_copy(
        src_ref=src,
        dst_ref=dst,
        send_sem=send_sem,
        recv_sem=recv_sem,
        device_id={"dom": dom, "mp": core},
        device_id_type=MESH,
    )


def aligned(index, size):
    if isinstance(index, int):
        return pl.ds(index * size, size)
    return pl.ds(pl.multiple_of(index * size, size), size)


def kernel(
    parts,
    col_ref,
    count_ref,
    send_ref,
    live_ref,
    recv_ref,
    feats_ref,
    tiles_in,
    cot_in,
    wg_in,
    wu_in,
    wd_in,
    final_out,
    fg_out,
    gg_out,
    gu_out,
    gd_out,
    idx_ref,
    tiles_ref,
    cot_ref,
    final_ref,
    fg_ref,
    gg_ref,
    gu_ref,
    gd_ref,
    adj,
    adj_t,
    own_pick,
    s_t,
    r_t,
    states,
    acts_t,
    hid_t,
    pre_g,
    pre_u,
    wg,
    wu,
    wd,
    wg_t,
    wu_t,
    wd_t,
    sbuf,
    halo,
    grads,
    res,
    p_one,
    p_sum,
    p_two,
    q_one,
    q_sum,
    q_two,
    h_send,
    h_recv,
    f_send,
    f_recv,
    w_send,
    w_recv,
    a_send,
    a_recv,
    i_sem,
    o_sem,
):
    me = lax.axis_index("dom")
    core = lax.axis_index("mp")
    sib = 1 - core
    layers = wg_in.shape[0]
    width = feats_ref.shape[1]
    units = wg_in.shape[2]
    rows = feats_ref.shape[0]
    blocks = rows // BLOCK
    tiles = rows // TILE
    slots = sbuf.shape[2]
    outer = parts // 2
    y = lax.rem(me, 2)
    z = me // 2
    f32, bf16 = jnp.float32, jnp.bfloat16

    def each_tile(body):
        for i in range(tiles):
            body(i, 0)

    barrier = pltpu.get_barrier_semaphore()

    def greet(i, _):
        q = lax.rem(me + i, parts)
        pl.semaphore_signal(
            barrier, inc=1, device_id={"dom": q, "mp": core}, device_id_type=MESH
        )
        return 0

    load_tiles = pltpu.make_async_copy(tiles_in, tiles_ref, i_sem.at[0])
    load_cot = pltpu.make_async_copy(cot_in, cot_ref, i_sem.at[1])
    load_weights = [
        pltpu.make_async_copy(src, dst.at[core], i_sem.at[2 + k])
        for k, (src, dst) in enumerate(((wg_in, wg), (wu_in, wu), (wd_in, wd)))
    ]
    lax.fori_loop(1, parts, greet, 0)
    pl.semaphore_signal(barrier, inc=1, device_id={"dom": me, "mp": sib}, device_id_type=MESH)

    for copy in load_weights:
        copy.start()
    load_tiles.start()
    load_cot.start()
    count = count_ref[0]

    def mask_of(i):
        index = lax.broadcasted_iota(jnp.int32, (TILE, 1), 0) + i * TILE
        return (index < count).astype(f32)

    def mask_rows(i, _):
        at = aligned(i, TILE)
        states[0, at, :] = (feats_ref[at, :].astype(f32) * mask_of(i)).astype(bf16)
        return 0

    each_tile(mask_rows)

    own_rows = parts * slots
    step = min(own_rows, TILE)
    slot = lax.broadcasted_iota(jnp.int32, (2 * slots, parts), 0)
    sources = jnp.where(slot < live_ref[...], jnp.transpose(send_ref[0]), -1)
    targets = jnp.transpose(recv_ref[0])

    def pick_rows(listed):
        for q in range(parts):
            column = listed[:, q : q + 1]
            column = jnp.where(core == 0, column[:slots], column[slots:])
            lane = lax.broadcasted_iota(jnp.int32, (slots, rows), 1)
            own_pick[q * slots : (q + 1) * slots, :] = (column == lane).astype(f32).astype(bf16)

    def lay_out(place, listed):
        pieces = [
            listed[h * slots : (h + 1) * slots, q : q + 1]
            for h in range(2)
            for q in range(parts)
        ]
        per = LANES // slots
        for k in range(0, len(pieces), per):
            column = jnp.concatenate(pieces[k : k + per], axis=0)
            across = jnp.transpose(jnp.broadcast_to(column, (LANES, LANES)))
            idx_ref[place : place + 1, k * slots : k * slots + LANES] = across[0:1, :]

    pick_rows(sources)
    pl.semaphore_wait(barrier, parts)

    def halo_send(phase, onehot, source):
        for begin in range(0, own_rows, step):
            picked = dot_nn(onehot[begin : begin + step, :], source[...]).astype(bf16)
            sbuf[phase, begin // slots : (begin + step) // slots] = picked.reshape(
                step // slots, slots, width
            )
        halo[phase, core, me] = sbuf[phase, me]

        def send(i, _):
            q = lax.rem(me + i, parts)
            remote(
                sbuf.at[phase, q],
                halo.at[phase, core, me],
                h_send.at[phase, q],
                h_recv.at[phase, me],
                q,
                core,
            ).start()
            return 0

        lax.fori_loop(1, parts, send, 0)
        forward(phase, me).start()

    def forward(phase, s):
        return remote(
            halo.at[phase, core, s],
            halo.at[phase, core, s],
            f_send.at[phase, s],
            f_recv.at[phase, s],
            me,
            sib,
        )

    def arrival(phase, s):
        return remote(
            sbuf.at[phase, s],
            halo.at[phase, core, s],
            h_send.at[phase, s],
            h_recv.at[phase, s],
            s,
            core,
        )

    def halo_recv(phase):
        def take(i, _):
            s = lax.rem(me + parts - i, parts)
            arrival(phase, s).wait_recv()
            forward(phase, s).start()
            return 0

        lax.fori_loop(1, parts, take, 0)

        def settle(s, _):
            remote(
                halo.at[phase, sib, s],
                halo.at[phase, sib, s],
                f_send.at[phase, s],
                f_recv.at[phase, s],
                me,
                sib,
            ).wait_recv()
            return 0

        lax.fori_loop(0, parts, settle, 0)

    def landed_rows(phase):
        return halo[phase].reshape(2 * own_rows, width)

    halo_send(0, own_pick, states.at[0])

    weight_copies = []
    for k, (src, dst) in enumerate(((wg_in, wg), (wu_in, wu), (wd_in, wd))):
        load_weights[k].wait()
        copy = remote(dst.at[core], dst.at[core], w_send.at[k], w_recv.at[k], me, sib)
        copy.start()
        weight_copies.append(copy)

    load_tiles.wait()
    lay_out(1, targets)

    def build(r, _):
        held = [col_ref[j, r] for j in range(tiles_ref.shape[1])]
        for c in range(blocks):
            j = jnp.int32(-1)
            for k, col in enumerate(held):
                j = jnp.where(col == c, k, j)
            tile = tiles_ref[r, jnp.maximum(j, 0)]
            adj[aligned(r, BLOCK), c * BLOCK : (c + 1) * BLOCK] = jnp.where(
                j >= 0, tile, jnp.zeros_like(tile)
            )
        return 0

    lax.fori_loop(0, blocks, build, 0)

    def build_send(i, _):
        at = aligned(i, TILE)
        index = lax.broadcasted_iota(jnp.int32, (TILE, 2 * own_rows), 0) + i * TILE
        s_t[at, :] = (idx_ref[0:1, :] == index).astype(f32).astype(bf16)
        return 0

    def build_receive(i, _):
        at = aligned(i, TILE)
        index = lax.broadcasted_iota(jnp.int32, (TILE, 2 * own_rows), 0) + i * TILE
        r_t[at, :] = (idx_ref[1:2, :] == index).astype(f32).astype(bf16)
        return 0

    def turn_tiles():
        def turn(r, _):
            for c in range(blocks):
                adj_t[c * BLOCK : (c + 1) * BLOCK, aligned(r, BLOCK)] = jnp.transpose(
                    adj[aligned(r, BLOCK), c * BLOCK : (c + 1) * BLOCK]
                )
            return 0

        lax.fori_loop(0, blocks, turn, 0)

    for layer in range(layers):
        if layer:
            halo_send(layer, own_pick, states.at[layer])
        state = states.at[layer]

        for begin in range(0, rows, 2 * TILE):
            at = pl.ds(begin, 2 * TILE)
            fg_ref[at, :] = dot_nn(adj[at, :], state[...])
        if layer == 0:
            each_tile(build_receive)
            for copy in weight_copies:
                copy.wait_recv()
        if layer == layers - 1:
            pick_rows(targets)
            lay_out(0, sources)
            each_tile(build_send)
            turn_tiles()
            for plain, turned in ((wg, wg_t), (wu, wu_t), (wd, wd_t)):
                for h in range(2):
                    for k in range(layers):
                        turned[h, k] = jnp.transpose(plain[h, k])
        halo_recv(layer)

        def mlp(i, _, layer=layer, state=state):
            at = aligned(i, TILE)
            act = (fg_ref[at, :] + dot_nn(r_t[at, :], landed_rows(layer))).astype(bf16)
            acts_t[layer, :, at] = jnp.transpose(act)
            made = []
            mixed = jnp.zeros((TILE, width), f32)
            for h in range(2):
                gate = dot_nn(act, wg[h, layer])
                up = dot_nn(act, wu[h, layer])
                sg = 0.5 * jnp.tanh(0.5 * gate) + 0.5
                silu = gate * sg
                hidden = (silu * up).astype(bf16)
                made.append(hidden)
                pre_g[layer, h, at, :] = (up * (sg * (1.0 + gate * (1.0 - sg)))).astype(bf16)
                pre_u[layer, h, at, :] = silu.astype(bf16)
                mixed = mixed + dot_nn(hidden, wd[h, layer])
            hid_t[layer, :, at] = jnp.transpose(jnp.where(core == 0, made[0], made[1]))
            new = ((state[at, :].astype(f32) + mixed) * mask_of(i)).astype(bf16)
            if layer + 1 < layers:
                states[layer + 1, at, :] = new
            else:
                final_ref[at, :] = new
            return 0

        each_tile(mlp)

    total = grads.shape[1]
    p_rows = total * 2 // 3
    p_half = p_rows // 2
    p_seg = p_half // outer
    q_seg = (total - p_rows) // outer
    q_half = q_seg // 2

    def at_rows(base, index, size):
        return pl.ds(pl.multiple_of(base + index * size, 16), size)

    def each_other(fn):
        def go(i, _):
            fn(lax.rem(z + i, outer))
            return 0

        lax.fori_loop(1, outer, go, 0)

    def pair(stage, layer, src, dst, slot):
        return remote(
            src,
            dst,
            a_send.at[layer, stage, outer + slot],
            a_recv.at[layer, stage, outer + slot],
            z * 2 + 1 - y,
            core,
        )

    def line(stage, layer, src, dst, to, slot, bank=0):
        return remote(
            src,
            dst,
            a_send.at[layer, stage, bank * outer + to],
            a_recv.at[layer, stage, bank * outer + slot],
            to * 2 + y,
            core,
        )

    def p_first(layer, t):
        return pair(
            0,
            layer,
            grads.at[layer, at_rows((1 - y) * p_half, t, p_seg)],
            p_one.at[layer, at_rows(0, t, p_seg)],
            t,
        )

    def p_added(layer, t):
        mine = grads[layer, at_rows(y * p_half, t, p_seg)].astype(f32)
        return (mine + p_one[layer, at_rows(0, t, p_seg)].astype(f32)).astype(bf16)

    def p_across(layer, t, slot):
        return line(
            1, layer, p_sum.at[layer, at_rows(0, t, p_seg)], p_two.at[layer, slot], t, slot
        )

    def p_spread(layer, owner, t, slot):
        place = res.at[layer, at_rows(y * p_half, owner, p_seg)]
        return line(2, layer, place, place, t, slot)

    def p_last(layer, half, t):
        place = res.at[layer, at_rows(half * p_half, t, p_seg)]
        return pair(3, layer, place, place, t)

    def q_first(layer, t, slot):
        return line(
            0,
            layer,
            grads.at[layer, at_rows(p_rows, t, q_seg)],
            q_one.at[layer, slot],
            t,
            slot,
        )

    def q_across(layer):
        source = q_sum.at[layer, at_rows(0, 1 - y, q_half)]
        return pair(1, layer, source, q_two.at[layer], 0)

    def q_spread(layer, half):
        place = res.at[layer, at_rows(p_rows + z * q_seg, half, q_half)]
        return pair(2, layer, place, place, 0)

    def q_last(layer, owner, half, t, slot, bank):
        place = res.at[layer, at_rows(p_rows + owner * q_seg, half, q_half)]
        return line(3, layer, place, place, t, slot, 2 * bank)

    def reduce_one(layer):
        def send(t):
            p_first(layer, t).start()
            q_first(layer, t, z).start()

        each_other(send)
        p_first(layer, z).start()
        q_one[layer, z] = grads[layer, at_rows(p_rows, z, q_seg)]

    def reduce_two(layer):
        def pass_on(t):
            p_first(layer, t).wait_recv()
            p_sum[layer, at_rows(0, t, p_seg)] = p_added(layer, t)
            p_across(layer, t, z).start()

        each_other(pass_on)
        p_first(layer, z).wait_recv()
        p_two[layer, z] = p_added(layer, z)
        each_other(lambda t: q_first(layer, t, t).wait_recv())
        q_sum[layer] = jnp.sum(q_one[layer].astype(f32), axis=0).astype(bf16)
        q_across(layer).start()

    def reduce_three(layer):
        each_other(lambda t: p_across(layer, t, t).wait_recv())
        res[layer, at_rows(y * p_half, z, p_seg)] = jnp.sum(
            p_two[layer].astype(f32), axis=0
        ).astype(bf16)
        each_other(lambda t: p_spread(layer, z, t, z).start())
        p_last(layer, y, z).start()
        q_across(layer).wait_recv()
        res[layer, at_rows(p_rows + z * q_seg, y, q_half)] = (
            q_sum[layer, at_rows(0, y, q_half)].astype(f32) + q_two[layer].astype(f32)
        ).astype(bf16)
        q_spread(layer, y).start()
        each_other(lambda t: q_last(layer, z, y, t, z, 0).start())

    def reduce_four(layer):
        q_spread(layer, 1 - y).wait_recv()

        def pass_on(t):
            p_spread(layer, t, t, t).wait_recv()
            p_last(layer, y, t).start()
            q_last(layer, z, 1 - y, t, z, 1).start()

        each_other(pass_on)

    def reduce_drain(layer):
        def sent(t):
            p_first(layer, t).wait_send()
            q_first(layer, t, z).wait_send()
            p_across(layer, t, z).wait_send()
            p_spread(layer, z, t, z).wait_send()
            p_last(layer, y, t).wait_send()
            q_last(layer, z, y, t, z, 0).wait_send()
            q_last(layer, z, 1 - y, t, z, 1).wait_send()

        each_other(sent)
        p_first(layer, z).wait_send()
        p_last(layer, y, z).wait_send()
        q_across(layer).wait_send()
        q_spread(layer, y).wait_send()

    def stores(layer):
        return [
            pltpu.make_async_copy(ref.at[layer], out.at[layer], o_sem.at[2 + k, layer])
            for k, (ref, out) in enumerate(((gg_ref, gg_out), (gu_ref, gu_out), (gd_ref, gd_out)))
        ]

    store_final = pltpu.make_async_copy(final_ref, final_out, o_sem.at[0, 0])
    store_final.start()
    store_fg = pltpu.make_async_copy(fg_ref, fg_out, o_sem.at[1, 0])

    def reduce_end(layer):
        def landed(t):
            p_last(layer, 1 - y, t).wait_recv()
            q_last(layer, t, y, t, t, 0).wait_recv()
            q_last(layer, t, 1 - y, t, t, 1).wait_recv()

        each_other(landed)
        p_last(layer, 1 - y, z).wait_recv()
        at = 0
        for out in (gg_ref, gu_ref, gd_ref):
            height, wide = out.shape[1:]
            for c in range(0, wide, LANES):
                out[layer, :, c : c + LANES] = res[layer, at : at + height].astype(f32)
                at += height
        for copy in stores(layer):
            copy.start()

    down_in, agg_grad = states.at[0], states.at[1]
    load_cot.wait()

    def start_rows(i, _):
        at = aligned(i, TILE)
        fg_ref[at, :] = cot_ref[at, :].astype(f32) * mask_of(i)
        return 0

    each_tile(start_rows)

    for layer in reversed(range(layers)):
        phase = 2 * layers - 1 - layer
        last = layer == layers - 1

        def mlp_back(i, _, layer=layer):
            at = aligned(i, TILE)
            down = fg_ref[at, :].astype(bf16)
            down_in[at, :] = down
            for h in range(2):
                hidden_grad = dot_nn(down, wd_t[h, layer])
                gate_grad = (hidden_grad * pre_g[layer, h, at, :].astype(f32)).astype(bf16)
                up_grad = (hidden_grad * pre_u[layer, h, at, :].astype(f32)).astype(bf16)
                pre_g[layer, h, at, :] = gate_grad
                pre_u[layer, h, at, :] = up_grad
            return 0

        def through_weights(i, _, layer=layer):
            at = aligned(i, TILE)
            total = jnp.zeros((TILE, width), f32)
            for h in range(2):
                total = total + dot_nn(pre_g[layer, h, at, :], wg_t[h, layer])
                total = total + dot_nn(pre_u[layer, h, at, :], wu_t[h, layer])
            agg_grad[at, :] = total.astype(bf16)
            return 0

        def weight_gradients(layer=layer):
            at = 0
            act = acts_t[layer]
            for left, right in (
                (act, pre_g[layer, core]),
                (act, pre_u[layer, core]),
                (hid_t[layer], down_in[...]),
            ):
                part = dot_nn(left, right).astype(bf16)
                for c in range(0, part.shape[1], LANES):
                    grads[layer, at : at + part.shape[0], :] = part[:, c : c + LANES]
                    at += part.shape[0]
            reduce_one(layer)

        each_tile(mlp_back)
        if layer == 0:
            weight_gradients()
            if not last:
                reduce_three(layer + 1)
        each_tile(through_weights)
        halo_send(phase, own_pick, agg_grad)
        if layer:
            if not last:
                reduce_three(layer + 1)
            weight_gradients()

        for begin in range(0, rows, 2 * TILE):
            at = pl.ds(begin, 2 * TILE)
            fg_ref[at, :] = fg_ref[at, :] + dot_nn(adj_t[at, :], agg_grad[...])
        if not last:
            reduce_two(layer)
        halo_recv(phase)
        if not last:
            reduce_four(layer + 1)

        def finish(i, _, phase=phase):
            at = aligned(i, TILE)
            fg_ref[at, :] = (fg_ref[at, :] + dot_nn(s_t[at, :], landed_rows(phase))) * mask_of(i)
            return 0

        each_tile(finish)
        if last:
            reduce_two(layer)

    store_fg.start()
    reduce_three(0)
    for layer in range(1, layers):
        reduce_end(layer)
    reduce_four(0)
    reduce_end(0)
    store_final.wait()
    store_fg.wait()
    for layer in range(layers):
        reduce_drain(layer)
        for copy in stores(layer):
            copy.wait()
    for copy in weight_copies:
        copy.wait_send()
    for phase in range(2 * layers):

        def drained(i, _, phase=phase):
            q = lax.rem(me + i, parts)
            arrival(phase, q).wait_send()
            forward(phase, q).wait_send()
            return 0

        lax.fori_loop(1, parts, drained, 0)
        forward(phase, me).wait_send()


def hand_over(*refs):
    count = (len(refs) - 2) // 3
    in_sem, out_sem = refs[-2:]
    pairs = []
    for k in range(count):
        source, target, held = refs[k], refs[count + k], refs[2 * count + k]
        cuts = 2 if source.shape[0] < 8 else 4
        size = source.shape[0] // cuts
        for cut in range(cuts):
            at = pl.ds(cut * size, size)
            pairs.append(
                (
                    pltpu.make_async_copy(source.at[at], held.at[at], in_sem.at[k, cut]),
                    pltpu.make_async_copy(held.at[at], target.at[at], out_sem.at[k, cut]),
                )
            )
    for load, _ in pairs:
        load.start()
    for load, store in pairs:
        load.wait()
        store.start()
    for _, store in pairs:
        store.wait()


def local(
    parts,
    feats,
    cell_count,
    tile_col,
    tile_val,
    send_list,
    send_count,
    recv_list,
    gate_weight_matrix,
    w_up,
    w_down,
    out_grad,
):
    rows, width = feats.shape
    layers, _, units = gate_weight_matrix.shape
    slot_count = send_list.shape[2]
    half = slot_count // 2
    outer = parts // 2
    all_slots = parts * slot_count
    total = 2 * width * (units // LANES) + units * (width // LANES)
    p_half = total // 3
    q_seg = (total - 2 * p_half) // outer
    f32, bf16 = jnp.float32, jnp.bfloat16
    vmem = pl.BlockSpec(memory_space=pltpu.VMEM)
    hbm = pl.BlockSpec(memory_space=pl.ANY)
    smem = pl.BlockSpec(memory_space=pltpu.SMEM)
    phases = 2 * layers
    dma = pltpu.SemaphoreType.DMA
    outs = pl.pallas_call(
        functools.partial(kernel, parts),
        out_shape=(
            jax.ShapeDtypeStruct((rows, width), bf16),
            jax.ShapeDtypeStruct((rows, width), f32),
            jax.ShapeDtypeStruct((layers, width, units), f32),
            jax.ShapeDtypeStruct((layers, width, units), f32),
            jax.ShapeDtypeStruct((layers, units, width), f32),
        ),
        in_specs=[smem, smem] + [vmem] * 4 + [hbm] * 5,
        out_specs=[hbm] * 5,
        scratch_shapes=[
            pltpu.VMEM((8, all_slots), jnp.int32),
            pltpu.VMEM(tile_val.shape, bf16),
            pltpu.VMEM((rows, width), bf16),
            pltpu.VMEM((rows, width), bf16),
            pltpu.VMEM((rows, width), f32),
            pltpu.VMEM((layers, width, units), f32),
            pltpu.VMEM((layers, width, units), f32),
            pltpu.VMEM((layers, units, width), f32),
            pltpu.VMEM((rows, rows), bf16),
            pltpu.VMEM((rows, rows), bf16),
            pltpu.VMEM((all_slots // 2, rows), bf16),
            pltpu.VMEM((rows, all_slots), bf16),
            pltpu.VMEM((rows, all_slots), bf16),
            pltpu.VMEM((max(layers, 2), rows, width), bf16),
            pltpu.VMEM((layers, width, rows), bf16),
            pltpu.VMEM((layers, units, rows), bf16),
            pltpu.VMEM((layers, 2, rows, units), bf16),
            pltpu.VMEM((layers, 2, rows, units), bf16),
            pltpu.VMEM((2, layers, width, units), bf16),
            pltpu.VMEM((2, layers, width, units), bf16),
            pltpu.VMEM((2, layers, units, width), bf16),
            pltpu.VMEM((2, layers, units, width), bf16),
            pltpu.VMEM((2, layers, units, width), bf16),
            pltpu.VMEM((2, layers, width, units), bf16),
            pltpu.VMEM((phases, parts, half, width), bf16),
            pltpu.VMEM((phases, 2, parts, half, width), bf16),
            pltpu.VMEM((layers, total, LANES), bf16),
            pltpu.VMEM((layers, total, LANES), bf16),
            pltpu.VMEM((layers, p_half, LANES), bf16),
            pltpu.VMEM((layers, p_half, LANES), bf16),
            pltpu.VMEM((layers, outer, p_half // outer, LANES), bf16),
            pltpu.VMEM((layers, outer, q_seg, LANES), bf16),
            pltpu.VMEM((layers, q_seg, LANES), bf16),
            pltpu.VMEM((layers, q_seg // 2, LANES), bf16),
            dma((phases, parts)),
            dma((phases, parts)),
            dma((phases, parts)),
            dma((phases, parts)),
            dma((3,)),
            dma((3,)),
            dma((layers, 4, 3 * outer)),
            dma((layers, 4, 3 * outer)),
            dma((5,)),
            dma((5, layers)),
        ],
        compiler_params=pltpu.CompilerParams(
            collective_id=0, has_side_effects=True, vmem_limit_bytes=60 * 1024 * 1024
        ),
        cost_estimate=pl.CostEstimate(
            flops=14 * 10**9, bytes_accessed=12 * 10**6, transcendentals=rows * units * 4
        ),
    )(
        jnp.transpose(tile_col),
        cell_count,
        send_list,
        send_count,
        recv_list,
        feats,
        tile_val,
        out_grad,
        gate_weight_matrix,
        w_up,
        w_down,
    )
    return pl.pallas_call(
        hand_over,
        out_shape=tuple(jax.ShapeDtypeStruct(out.shape, out.dtype) for out in outs),
        in_specs=[hbm] * len(outs),
        out_specs=[hbm] * len(outs),
        scratch_shapes=[pltpu.VMEM(out.shape, out.dtype) for out in outs]
        + [dma((len(outs), 4)), dma((len(outs), 4))],
        compiler_params=pltpu.CompilerParams(vmem_limit_bytes=60 * 1024 * 1024),
    )(*outs)


def solution(mesh):
    return jax.shard_map(
        functools.partial(local, mesh.shape["dom"]),
        mesh=mesh,
        in_specs=(
            P(("groups", "dom"), None),
            P(("groups", "dom")),
            P(("groups", "dom"), None),
            P(("groups", "dom"), None, None, None),
            P(("groups", "dom"), None, None),
            P(("groups", "dom"), None),
            P(("groups", "dom"), None, None),
            P(None, None, "mp"),
            P(None, None, "mp"),
            P(None, "mp", None),
            P(("groups", "dom"), None),
        ),
        out_specs=(
            P(("groups", "dom"), None),
            P(("groups", "dom"), None),
            P("groups", None, "mp"),
            P("groups", None, "mp"),
            P("groups", "mp", None),
        ),
        check_vma=False,
    )
```

```python
import functools

import jax
import jax.numpy as jnp
from jax import lax
from jax.experimental import pallas as pl
from jax.experimental.pallas import tpu as pltpu
from jax.sharding import PartitionSpec as P

MESH = pl.DeviceIdType.MESH
BLOCK = 128
LANES = 128
TILE = 256


def dot_nn(left, right):
    return lax.dot_general(
        left, right, (((1,), (0,)), ((), ())), preferred_element_type=jnp.float32
    )


def remote(src, dst, send_sem, recv_sem, dom, core):
    return pltpu.make_async_remote_copy(
        src_ref=src,
        dst_ref=dst,
        send_sem=send_sem,
        recv_sem=recv_sem,
        device_id={"dom": dom, "mp": core},
        device_id_type=MESH,
    )


def aligned(index, size):
    if isinstance(index, int):
        return pl.ds(index * size, size)
    return pl.ds(pl.multiple_of(index * size, size), size)


def kernel(
    parts,
    col_ref,
    count_ref,
    send_ref,
    live_ref,
    recv_ref,
    feats_ref,
    tiles_in,
    cot_in,
    wg_in,
    wu_in,
    wd_in,
    final_out,
    fg_out,
    gg_out,
    gu_out,
    gd_out,
    idx_ref,
    tiles_ref,
    cot_ref,
    final_ref,
    fg_ref,
    gg_ref,
    gu_ref,
    gd_ref,
    adj,
    adj_t,
    own_pick,
    s_t,
    r_t,
    states,
    acts_t,
    hid_t,
    pre_g,
    pre_u,
    wg,
    wu,
    wd,
    wg_t,
    wu_t,
    wd_t,
    sbuf,
    halo,
    grads,
    res,
    p_one,
    p_sum,
    p_two,
    q_one,
    q_sum,
    q_two,
    h_send,
    h_recv,
    f_send,
    f_recv,
    w_send,
    w_recv,
    a_send,
    a_recv,
    i_sem,
    o_sem,
    inv_ref,
):
    me = lax.axis_index("dom")
    core = lax.axis_index("mp")
    sib = 1 - core
    layers = wg_in.shape[0]
    width = feats_ref.shape[1]
    units = wg_in.shape[2]
    rows = feats_ref.shape[0]
    blocks = rows // BLOCK
    tiles = rows // TILE
    slots = sbuf.shape[2]
    outer = parts // 2
    y = lax.rem(me, 2)
    z = me // 2
    f32, bf16 = jnp.float32, jnp.bfloat16

    def each_tile(body):
        for i in range(tiles):
            body(i, 0)

    barrier = pltpu.get_barrier_semaphore()

    def greet(i, _):
        q = lax.rem(me + i, parts)
        pl.semaphore_signal(
            barrier, inc=1, device_id={"dom": q, "mp": core}, device_id_type=MESH
        )
        return 0

    load_tiles = pltpu.make_async_copy(tiles_in, tiles_ref, i_sem.at[0])
    load_cot = pltpu.make_async_copy(cot_in, cot_ref, i_sem.at[1])
    load_weights = [
        pltpu.make_async_copy(src, dst.at[core], i_sem.at[2 + k])
        for k, (src, dst) in enumerate(((wg_in, wg), (wu_in, wu), (wd_in, wd)))
    ]
    lax.fori_loop(1, parts, greet, 0)
    pl.semaphore_signal(barrier, inc=1, device_id={"dom": me, "mp": sib}, device_id_type=MESH)

    for copy in load_weights:
        copy.start()
    load_tiles.start()
    load_cot.start()
    count = count_ref[0]

    def mask_of(i):
        index = lax.broadcasted_iota(jnp.int32, (TILE, 1), 0) + i * TILE
        return (index < count).astype(f32)

    def mask_rows(i, _):
        at = aligned(i, TILE)
        states[0, at, :] = (feats_ref[at, :].astype(f32) * mask_of(i)).astype(bf16)
        return 0

    each_tile(mask_rows)

    own_rows = parts * slots
    step = min(own_rows, TILE)
    slot = lax.broadcasted_iota(jnp.int32, (2 * slots, parts), 0)
    sources = jnp.where(slot < live_ref[...], jnp.transpose(send_ref[0]), -1)
    targets = jnp.transpose(recv_ref[0])

    def pick_rows(listed):
        for q in range(parts):
            column = listed[:, q : q + 1]
            column = jnp.where(core == 0, column[:slots], column[slots:])
            lane = lax.broadcasted_iota(jnp.int32, (slots, rows), 1)
            own_pick[q * slots : (q + 1) * slots, :] = (column == lane).astype(f32).astype(bf16)

    def lay_out(place, listed):
        pieces = [
            listed[h * slots : (h + 1) * slots, q : q + 1]
            for h in range(2)
            for q in range(parts)
        ]
        per = LANES // slots
        for k in range(0, len(pieces), per):
            column = jnp.concatenate(pieces[k : k + per], axis=0)
            across = jnp.transpose(jnp.broadcast_to(column, (LANES, LANES)))
            idx_ref[place : place + 1, k * slots : k * slots + LANES] = across[0:1, :]

    pick_rows(sources)
    def halo_pick(phase, onehot, source):
        for begin in range(0, own_rows, step):
            picked = dot_nn(onehot[begin : begin + step, :], source[...]).astype(bf16)
            sbuf[phase, begin // slots : (begin + step) // slots] = picked.reshape(
                step // slots, slots, width
            )
        halo[phase, core, me] = sbuf[phase, me]

    def halo_send(phase):
        def send(i, _):
            q = lax.rem(me + i, parts)
            remote(
                sbuf.at[phase, q],
                halo.at[phase, core, me],
                h_send.at[phase, q],
                h_recv.at[phase, me],
                q,
                core,
            ).start()
            return 0

        lax.fori_loop(1, parts, send, 0)
        forward(phase, me).start()

    def forward(phase, s):
        return remote(
            halo.at[phase, core, s],
            halo.at[phase, core, s],
            f_send.at[phase, s],
            f_recv.at[phase, s],
            me,
            sib,
        )

    def arrival(phase, s):
        return remote(
            sbuf.at[phase, s],
            halo.at[phase, core, s],
            h_send.at[phase, s],
            h_recv.at[phase, s],
            s,
            core,
        )

    def halo_recv(phase):
        def take(i, _):
            s = lax.rem(me + parts - i, parts)
            arrival(phase, s).wait_recv()
            forward(phase, s).start()
            return 0

        lax.fori_loop(1, parts, take, 0)

        def settle(s, _):
            remote(
                halo.at[phase, sib, s],
                halo.at[phase, sib, s],
                f_send.at[phase, s],
                f_recv.at[phase, s],
                me,
                sib,
            ).wait_recv()
            return 0

        lax.fori_loop(0, parts, settle, 0)

    def landed_rows(phase):
        return halo[phase].reshape(2 * own_rows, width)

    halo_pick(0, own_pick, states.at[0])
    pl.semaphore_wait(barrier, parts)
    halo_send(0)

    weight_copies = []
    for k, (src, dst) in enumerate(((wg_in, wg), (wu_in, wu), (wd_in, wd))):
        load_weights[k].wait()
        copy = remote(dst.at[core], dst.at[core], w_send.at[k], w_recv.at[k], me, sib)
        copy.start()
        weight_copies.append(copy)

    load_tiles.wait()
    lay_out(1, targets)

    def build(r, _):
        held = [col_ref[j, r] for j in range(tiles_ref.shape[1])]
        for c in range(blocks):
            j = jnp.int32(-1)
            for k, col in enumerate(held):
                j = jnp.where(col == c, k, j)
            inv_ref[r, c] = j
            tile = tiles_ref[r, jnp.maximum(j, 0)]
            adj[aligned(r, BLOCK), c * BLOCK : (c + 1) * BLOCK] = jnp.where(
                j >= 0, tile, jnp.zeros_like(tile)
            )
        return 0

    lax.fori_loop(0, blocks, build, 0)

    def build_send(i, _):
        at = aligned(i, TILE)
        index = lax.broadcasted_iota(jnp.int32, (TILE, 2 * own_rows), 0) + i * TILE
        s_t[at, :] = (idx_ref[0:1, :] == index).astype(f32).astype(bf16)
        return 0

    def build_receive(i, _):
        at = aligned(i, TILE)
        index = lax.broadcasted_iota(jnp.int32, (TILE, 2 * own_rows), 0) + i * TILE
        r_t[at, :] = (idx_ref[1:2, :] == index).astype(f32).astype(bf16)
        return 0

    def place_turned():
        def turn(r, _):
            for c in range(blocks):
                j = inv_ref[r, c]
                tile = tiles_ref[r, jnp.maximum(j, 0)]
                adj_t[c * BLOCK : (c + 1) * BLOCK, aligned(r, BLOCK)] = jnp.where(
                    j >= 0, tile, jnp.zeros_like(tile)
                )
            return 0

        lax.fori_loop(0, blocks, turn, 0)

    def turn_share(part, whole):
        for r in range(part * blocks // whole, (part + 1) * blocks // whole):
            for j in range(tiles_ref.shape[1]):
                tiles_ref[r, j] = jnp.transpose(tiles_ref[r, j])

    for layer in range(layers):
        if layer:
            halo_pick(layer, own_pick, states.at[layer])
            halo_send(layer)
        state = states.at[layer]

        for begin in range(0, rows, 2 * TILE):
            at = pl.ds(begin, 2 * TILE)
            fg_ref[at, :] = dot_nn(adj[at, :], state[...])
        if layer == 0:
            each_tile(build_receive)
            for copy in weight_copies:
                copy.wait_recv()
        if layer == layers - 1:
            pick_rows(targets)
            lay_out(0, sources)
            each_tile(build_send)
            for plain, turned in ((wg, wg_t), (wu, wu_t), (wd, wd_t)):
                for h in range(2):
                    for k in range(layers):
                        turned[h, k] = jnp.transpose(plain[h, k])
        halo_recv(layer)

        def mlp(i, _, layer=layer, state=state):
            at = aligned(i, TILE)
            turn_share(layer * tiles + i, layers * tiles)
            act = (fg_ref[at, :] + dot_nn(r_t[at, :], landed_rows(layer))).astype(bf16)
            acts_t[layer, :, at] = jnp.transpose(act)
            made = []
            mixed = jnp.zeros((TILE, width), f32)
            for h in range(2):
                gate = dot_nn(act, wg[h, layer])
                up = dot_nn(act, wu[h, layer])
                sg = 0.5 * jnp.tanh(0.5 * gate) + 0.5
                silu = gate * sg
                hidden = (silu * up).astype(bf16)
                made.append(hidden)
                pre_g[layer, h, at, :] = (up * (sg * (1.0 + gate * (1.0 - sg)))).astype(bf16)
                pre_u[layer, h, at, :] = silu.astype(bf16)
                mixed = mixed + dot_nn(hidden, wd[h, layer])
            hid_t[layer, :, at] = jnp.transpose(jnp.where(core == 0, made[0], made[1]))
            new = ((state[at, :].astype(f32) + mixed) * mask_of(i)).astype(bf16)
            if layer + 1 < layers:
                states[layer + 1, at, :] = new
            else:
                final_ref[at, :] = new
            return 0

        each_tile(mlp)

    total = grads.shape[1]
    p_rows = total * 2 // 3
    p_half = p_rows // 2
    p_seg = p_half // outer
    q_seg = (total - p_rows) // outer
    q_half = q_seg // 2

    def at_rows(base, index, size):
        return pl.ds(pl.multiple_of(base + index * size, 16), size)

    def each_other(fn):
        def go(i, _):
            fn(lax.rem(z + i, outer))
            return 0

        lax.fori_loop(1, outer, go, 0)

    def pair(stage, layer, src, dst, slot):
        return remote(
            src,
            dst,
            a_send.at[layer, stage, outer + slot],
            a_recv.at[layer, stage, outer + slot],
            z * 2 + 1 - y,
            core,
        )

    def line(stage, layer, src, dst, to, slot, bank=0):
        return remote(
            src,
            dst,
            a_send.at[layer, stage, bank * outer + to],
            a_recv.at[layer, stage, bank * outer + slot],
            to * 2 + y,
            core,
        )

    def p_first(layer, t):
        return pair(
            0,
            layer,
            grads.at[layer, at_rows((1 - y) * p_half, t, p_seg)],
            p_one.at[layer, at_rows(0, t, p_seg)],
            t,
        )

    def p_added(layer, t):
        mine = grads[layer, at_rows(y * p_half, t, p_seg)].astype(f32)
        return (mine + p_one[layer, at_rows(0, t, p_seg)].astype(f32)).astype(bf16)

    def p_across(layer, t, slot):
        return line(
            1, layer, p_sum.at[layer, at_rows(0, t, p_seg)], p_two.at[layer, slot], t, slot
        )

    def p_spread(layer, owner, t, slot):
        place = res.at[layer, at_rows(y * p_half, owner, p_seg)]
        return line(2, layer, place, place, t, slot)

    def p_last(layer, half, t):
        place = res.at[layer, at_rows(half * p_half, t, p_seg)]
        return pair(3, layer, place, place, t)

    def q_first(layer, t, slot):
        return line(
            0,
            layer,
            grads.at[layer, at_rows(p_rows, t, q_seg)],
            q_one.at[layer, slot],
            t,
            slot,
        )

    def q_across(layer):
        source = q_sum.at[layer, at_rows(0, 1 - y, q_half)]
        return pair(1, layer, source, q_two.at[layer], 0)

    def q_spread(layer, half):
        place = res.at[layer, at_rows(p_rows + z * q_seg, half, q_half)]
        return pair(2, layer, place, place, 0)

    def q_last(layer, owner, half, t, slot, bank):
        place = res.at[layer, at_rows(p_rows + owner * q_seg, half, q_half)]
        return line(3, layer, place, place, t, slot, 2 * bank)

    def reduce_one(layer):
        def send(t):
            p_first(layer, t).start()
            q_first(layer, t, z).start()

        each_other(send)
        p_first(layer, z).start()
        q_one[layer, z] = grads[layer, at_rows(p_rows, z, q_seg)]

    def reduce_two(layer):
        def pass_on(t):
            p_first(layer, t).wait_recv()
            p_sum[layer, at_rows(0, t, p_seg)] = p_added(layer, t)
            p_across(layer, t, z).start()

        each_other(pass_on)
        p_first(layer, z).wait_recv()
        p_two[layer, z] = p_added(layer, z)
        each_other(lambda t: q_first(layer, t, t).wait_recv())
        q_sum[layer] = jnp.sum(q_one[layer].astype(f32), axis=0).astype(bf16)
        q_across(layer).start()

    def reduce_three(layer):
        each_other(lambda t: p_across(layer, t, t).wait_recv())
        res[layer, at_rows(y * p_half, z, p_seg)] = jnp.sum(
            p_two[layer].astype(f32), axis=0
        ).astype(bf16)
        each_other(lambda t: p_spread(layer, z, t, z).start())
        p_last(layer, y, z).start()
        q_across(layer).wait_recv()
        res[layer, at_rows(p_rows + z * q_seg, y, q_half)] = (
            q_sum[layer, at_rows(0, y, q_half)].astype(f32) + q_two[layer].astype(f32)
        ).astype(bf16)
        q_spread(layer, y).start()
        each_other(lambda t: q_last(layer, z, y, t, z, 0).start())

    def reduce_four(layer):
        q_spread(layer, 1 - y).wait_recv()

        def pass_on(t):
            p_spread(layer, t, t, t).wait_recv()
            p_last(layer, y, t).start()
            q_last(layer, z, 1 - y, t, z, 1).start()

        each_other(pass_on)

    def reduce_drain(layer):
        def sent(t):
            p_first(layer, t).wait_send()
            q_first(layer, t, z).wait_send()
            p_across(layer, t, z).wait_send()
            p_spread(layer, z, t, z).wait_send()
            p_last(layer, y, t).wait_send()
            q_last(layer, z, y, t, z, 0).wait_send()
            q_last(layer, z, 1 - y, t, z, 1).wait_send()

        each_other(sent)
        p_first(layer, z).wait_send()
        p_last(layer, y, z).wait_send()
        q_across(layer).wait_send()
        q_spread(layer, y).wait_send()

    def stores(layer):
        return [
            pltpu.make_async_copy(ref.at[layer], out.at[layer], o_sem.at[2 + k, layer])
            for k, (ref, out) in enumerate(((gg_ref, gg_out), (gu_ref, gu_out), (gd_ref, gd_out)))
        ]

    store_final = pltpu.make_async_copy(final_ref, final_out, o_sem.at[0, 0])
    store_final.start()
    store_fg = pltpu.make_async_copy(fg_ref, fg_out, o_sem.at[1, 0])

    def reduce_end(layer):
        def landed(t):
            p_last(layer, 1 - y, t).wait_recv()
            q_last(layer, t, y, t, t, 0).wait_recv()
            q_last(layer, t, 1 - y, t, t, 1).wait_recv()

        each_other(landed)
        p_last(layer, 1 - y, z).wait_recv()
        at = 0
        for out in (gg_ref, gu_ref, gd_ref):
            height, wide = out.shape[1:]
            for c in range(0, wide, LANES):
                out[layer, :, c : c + LANES] = res[layer, at : at + height].astype(f32)
                at += height
        for copy in stores(layer):
            copy.start()

    down_in, agg_grad = states.at[0], states.at[1]
    load_cot.wait()

    def start_rows(i, _):
        at = aligned(i, TILE)
        fg_ref[at, :] = cot_ref[at, :].astype(f32) * mask_of(i)
        return 0

    each_tile(start_rows)

    for layer in reversed(range(layers)):
        phase = 2 * layers - 1 - layer
        last = layer == layers - 1

        def mlp_back(i, _, layer=layer):
            at = aligned(i, TILE)
            down = fg_ref[at, :].astype(bf16)
            down_in[at, :] = down
            for h in range(2):
                hidden_grad = dot_nn(down, wd_t[h, layer])
                gate_grad = (hidden_grad * pre_g[layer, h, at, :].astype(f32)).astype(bf16)
                up_grad = (hidden_grad * pre_u[layer, h, at, :].astype(f32)).astype(bf16)
                pre_g[layer, h, at, :] = gate_grad
                pre_u[layer, h, at, :] = up_grad
            return 0

        def through_weights(i, _, layer=layer):
            at = aligned(i, TILE)
            total = jnp.zeros((TILE, width), f32)
            for h in range(2):
                total = total + dot_nn(pre_g[layer, h, at, :], wg_t[h, layer])
                total = total + dot_nn(pre_u[layer, h, at, :], wu_t[h, layer])
            agg_grad[at, :] = total.astype(bf16)
            return 0

        def weight_gradients(layer=layer):
            at = 0
            act = acts_t[layer]
            for left, right in (
                (act, pre_g[layer, core]),
                (act, pre_u[layer, core]),
                (hid_t[layer], down_in[...]),
            ):
                part = dot_nn(left, right).astype(bf16)
                for c in range(0, part.shape[1], LANES):
                    grads[layer, at : at + part.shape[0], :] = part[:, c : c + LANES]
                    at += part.shape[0]
            reduce_one(layer)

        each_tile(mlp_back)
        if layer == 0:
            weight_gradients()
            if not last:
                reduce_three(layer + 1)
        each_tile(through_weights)
        halo_pick(phase, own_pick, agg_grad)
        halo_send(phase)
        if layer:
            if not last:
                reduce_three(layer + 1)
            weight_gradients()
        if last:
            place_turned()

        for begin in range(0, rows, 2 * TILE):
            at = pl.ds(begin, 2 * TILE)
            fg_ref[at, :] = fg_ref[at, :] + dot_nn(adj_t[at, :], agg_grad[...])
        if not last:
            reduce_two(layer)
        halo_recv(phase)
        if not last:
            reduce_four(layer + 1)

        def finish(i, _, phase=phase):
            at = aligned(i, TILE)
            fg_ref[at, :] = (fg_ref[at, :] + dot_nn(s_t[at, :], landed_rows(phase))) * mask_of(i)
            return 0

        each_tile(finish)
        if last:
            reduce_two(layer)

    store_fg.start()
    reduce_three(0)
    for layer in range(1, layers):
        reduce_end(layer)
    reduce_four(0)
    reduce_end(0)
    store_final.wait()
    store_fg.wait()
    for layer in range(layers):
        reduce_drain(layer)
        for copy in stores(layer):
            copy.wait()
    for copy in weight_copies:
        copy.wait_send()
    for phase in range(2 * layers):

        def drained(i, _, phase=phase):
            q = lax.rem(me + i, parts)
            arrival(phase, q).wait_send()
            forward(phase, q).wait_send()
            return 0

        lax.fori_loop(1, parts, drained, 0)
        forward(phase, me).wait_send()


def hand_over(*refs):
    count = (len(refs) - 2) // 3
    in_sem, out_sem = refs[-2:]
    pairs = []
    for k in range(count):
        source, target, held = refs[k], refs[count + k], refs[2 * count + k]
        cuts = 2 if source.shape[0] < 8 else 4
        size = source.shape[0] // cuts
        for cut in range(cuts):
            at = pl.ds(cut * size, size)
            pairs.append(
                (
                    pltpu.make_async_copy(source.at[at], held.at[at], in_sem.at[k, cut]),
                    pltpu.make_async_copy(held.at[at], target.at[at], out_sem.at[k, cut]),
                )
            )
    for load, _ in pairs:
        load.start()
    for load, store in pairs:
        load.wait()
        store.start()
    for _, store in pairs:
        store.wait()


def local(
    parts,
    feats,
    cell_count,
    tile_col,
    tile_val,
    send_list,
    send_count,
    recv_list,
    gate_weight_matrix,
    w_up,
    w_down,
    out_grad,
):
    rows, width = feats.shape
    layers, _, units = gate_weight_matrix.shape
    slot_count = send_list.shape[2]
    half = slot_count // 2
    outer = parts // 2
    all_slots = parts * slot_count
    total = 2 * width * (units // LANES) + units * (width // LANES)
    p_half = total // 3
    q_seg = (total - 2 * p_half) // outer
    f32, bf16 = jnp.float32, jnp.bfloat16
    vmem = pl.BlockSpec(memory_space=pltpu.VMEM)
    hbm = pl.BlockSpec(memory_space=pl.ANY)
    smem = pl.BlockSpec(memory_space=pltpu.SMEM)
    phases = 2 * layers
    dma = pltpu.SemaphoreType.DMA
    outs = pl.pallas_call(
        functools.partial(kernel, parts),
        out_shape=(
            jax.ShapeDtypeStruct((rows, width), bf16),
            jax.ShapeDtypeStruct((rows, width), f32),
            jax.ShapeDtypeStruct((layers, width, units), f32),
            jax.ShapeDtypeStruct((layers, width, units), f32),
            jax.ShapeDtypeStruct((layers, units, width), f32),
        ),
        in_specs=[smem, smem] + [vmem] * 4 + [pl.BlockSpec(memory_space=pltpu.HBM)] * 5,
        out_specs=[hbm] * 5,
        scratch_shapes=[
            pltpu.VMEM((8, all_slots), jnp.int32),
            pltpu.VMEM(tile_val.shape, bf16),
            pltpu.VMEM((rows, width), bf16),
            pltpu.VMEM((rows, width), bf16),
            pltpu.VMEM((rows, width), f32),
            pltpu.VMEM((layers, width, units), f32),
            pltpu.VMEM((layers, width, units), f32),
            pltpu.VMEM((layers, units, width), f32),
            pltpu.VMEM((rows, rows), bf16),
            pltpu.VMEM((rows, rows), bf16),
            pltpu.VMEM((all_slots // 2, rows), bf16),
            pltpu.VMEM((rows, all_slots), bf16),
            pltpu.VMEM((rows, all_slots), bf16),
            pltpu.VMEM((max(layers, 2), rows, width), bf16),
            pltpu.VMEM((layers, width, rows), bf16),
            pltpu.VMEM((layers, units, rows), bf16),
            pltpu.VMEM((layers, 2, rows, units), bf16),
            pltpu.VMEM((layers, 2, rows, units), bf16),
            pltpu.VMEM((2, layers, width, units), bf16),
            pltpu.VMEM((2, layers, width, units), bf16),
            pltpu.VMEM((2, layers, units, width), bf16),
            pltpu.VMEM((2, layers, units, width), bf16),
            pltpu.VMEM((2, layers, units, width), bf16),
            pltpu.VMEM((2, layers, width, units), bf16),
            pltpu.VMEM((phases, parts, half, width), bf16),
            pltpu.VMEM((phases, 2, parts, half, width), bf16),
            pltpu.VMEM((layers, total, LANES), bf16),
            pltpu.VMEM((layers, total, LANES), bf16),
            pltpu.VMEM((layers, p_half, LANES), bf16),
            pltpu.VMEM((layers, p_half, LANES), bf16),
            pltpu.VMEM((layers, outer, p_half // outer, LANES), bf16),
            pltpu.VMEM((layers, outer, q_seg, LANES), bf16),
            pltpu.VMEM((layers, q_seg, LANES), bf16),
            pltpu.VMEM((layers, q_seg // 2, LANES), bf16),
            dma((phases, parts)),
            dma((phases, parts)),
            dma((phases, parts)),
            dma((phases, parts)),
            dma((3,)),
            dma((3,)),
            dma((layers, 4, 3 * outer)),
            dma((layers, 4, 3 * outer)),
            dma((5,)),
            dma((5, layers)),
            pltpu.SMEM((rows // BLOCK, rows // BLOCK), jnp.int32),
        ],
        compiler_params=pltpu.CompilerParams(
            collective_id=0, has_side_effects=True, vmem_limit_bytes=min(60, 44 + parts // 2) * 1024 * 1024
        ),
        cost_estimate=pl.CostEstimate(
            flops=14 * 10**9, bytes_accessed=12 * 10**6, transcendentals=rows * units * 4
        ),
    )(
        jnp.transpose(tile_col),
        cell_count,
        send_list,
        send_count,
        recv_list,
        feats,
        tile_val,
        out_grad,
        gate_weight_matrix,
        w_up,
        w_down,
    )
    return pl.pallas_call(
        hand_over,
        out_shape=tuple(jax.ShapeDtypeStruct(out.shape, out.dtype) for out in outs),
        in_specs=[hbm] * len(outs),
        out_specs=[hbm] * len(outs),
        scratch_shapes=[pltpu.VMEM(out.shape, out.dtype) for out in outs]
        + [dma((len(outs), 4)), dma((len(outs), 4))],
        compiler_params=pltpu.CompilerParams(vmem_limit_bytes=8 * 1024 * 1024),
    )(*outs)


def solution(mesh):
    return jax.shard_map(
        functools.partial(local, mesh.shape["dom"]),
        mesh=mesh,
        in_specs=(
            P(("groups", "dom"), None),
            P(("groups", "dom")),
            P(("groups", "dom"), None),
            P(("groups", "dom"), None, None, None),
            P(("groups", "dom"), None, None),
            P(("groups", "dom"), None),
            P(("groups", "dom"), None, None),
            P(None, None, "mp"),
            P(None, None, "mp"),
            P(None, "mp", None),
            P(("groups", "dom"), None),
        ),
        out_specs=(
            P(("groups", "dom"), None),
            P(("groups", "dom"), None),
            P("groups", None, "mp"),
            P("groups", None, "mp"),
            P("groups", "mp", None),
        ),
        check_vma=False,
    )
```

```python
import functools

import jax
import jax.numpy as jnp
from jax import lax
from jax.experimental import pallas as pl
from jax.experimental.pallas import tpu as pltpu
from jax.sharding import PartitionSpec as P

MESH = pl.DeviceIdType.MESH
BLOCK = 128
LANES = 128
TILE = 256


def dot_nn(left, right):
    return lax.dot_general(
        left, right, (((1,), (0,)), ((), ())), preferred_element_type=jnp.float32
    )


def remote(src, dst, send_sem, recv_sem, dom, core):
    return pltpu.make_async_remote_copy(
        src_ref=src,
        dst_ref=dst,
        send_sem=send_sem,
        recv_sem=recv_sem,
        device_id={"dom": dom, "mp": core},
        device_id_type=MESH,
    )


def aligned(index, size):
    if isinstance(index, int):
        return pl.ds(index * size, size)
    return pl.ds(pl.multiple_of(index * size, size), size)


def kernel(
    parts,
    col_ref,
    count_ref,
    send_ref,
    live_ref,
    recv_ref,
    feats_ref,
    tiles_in,
    cot_in,
    wg_in,
    wu_in,
    wd_in,
    final_out,
    fg_out,
    gg_out,
    gu_out,
    gd_out,
    idx_ref,
    tiles_ref,
    cot_ref,
    final_ref,
    fg_ref,
    gg_ref,
    gu_ref,
    gd_ref,
    adj,
    adj_t,
    own_pick,
    s_t,
    r_t,
    states,
    acts_t,
    hid_t,
    pre_g,
    pre_u,
    wg,
    wu,
    wd,
    wg_t,
    wu_t,
    wd_t,
    sbuf,
    halo,
    grads,
    res,
    p_one,
    p_sum,
    p_two,
    q_one,
    q_sum,
    q_two,
    h_send,
    h_recv,
    f_send,
    f_recv,
    w_send,
    w_recv,
    a_send,
    a_recv,
    i_sem,
    o_sem,
    inv_ref,
):
    me = lax.axis_index("dom")
    core = lax.axis_index("mp")
    sib = 1 - core
    layers = wg_in.shape[0]
    width = feats_ref.shape[1]
    units = wg_in.shape[2]
    rows = feats_ref.shape[0]
    blocks = rows // BLOCK
    tiles = rows // TILE
    slots = sbuf.shape[2]
    outer = parts // 2
    y = lax.rem(me, 2)
    z = me // 2
    f32, bf16 = jnp.float32, jnp.bfloat16

    def each_tile(body):
        for i in range(tiles):
            body(i, 0)

    barrier = pltpu.get_barrier_semaphore()

    def greet(i, _):
        q = lax.rem(me + i, parts)
        pl.semaphore_signal(
            barrier, inc=1, device_id={"dom": q, "mp": core}, device_id_type=MESH
        )
        return 0

    load_tiles = pltpu.make_async_copy(tiles_in, tiles_ref, i_sem.at[0])
    load_cot = pltpu.make_async_copy(cot_in, cot_ref, i_sem.at[1])
    load_weights = [
        pltpu.make_async_copy(src, dst.at[core], i_sem.at[2 + k])
        for k, (src, dst) in enumerate(((wg_in, wg), (wu_in, wu), (wd_in, wd)))
    ]
    lax.fori_loop(1, parts, greet, 0)
    pl.semaphore_signal(barrier, inc=1, device_id={"dom": me, "mp": sib}, device_id_type=MESH)

    for copy in load_weights:
        copy.start()
    load_tiles.start()
    load_cot.start()
    count = count_ref[0]

    def mask_of(i):
        index = lax.broadcasted_iota(jnp.int32, (TILE, 1), 0) + i * TILE
        return (index < count).astype(f32)

    def mask_rows(i, _):
        at = aligned(i, TILE)
        states[0, at, :] = (feats_ref[at, :].astype(f32) * mask_of(i)).astype(bf16)
        return 0

    each_tile(mask_rows)

    own_rows = parts * slots
    step = min(own_rows, TILE)
    slot = lax.broadcasted_iota(jnp.int32, (2 * slots, parts), 0)
    sources = jnp.where(slot < live_ref[...], jnp.transpose(send_ref[0]), -1)
    targets = jnp.transpose(recv_ref[0])

    def pick_rows(listed):
        for q in range(parts):
            column = listed[:, q : q + 1]
            column = jnp.where(core == 0, column[:slots], column[slots:])
            lane = lax.broadcasted_iota(jnp.int32, (slots, rows), 1)
            own_pick[q * slots : (q + 1) * slots, :] = (column == lane).astype(f32).astype(bf16)

    def lay_out(place, listed):
        pieces = [
            listed[h * slots : (h + 1) * slots, q : q + 1]
            for h in range(2)
            for q in range(parts)
        ]
        per = LANES // slots
        for k in range(0, len(pieces), per):
            column = jnp.concatenate(pieces[k : k + per], axis=0)
            across = jnp.transpose(jnp.broadcast_to(column, (LANES, LANES)))
            idx_ref[place : place + 1, k * slots : k * slots + LANES] = across[0:1, :]

    pick_rows(sources)
    def halo_pick(phase, onehot, source):
        for begin in range(0, own_rows, step):
            picked = dot_nn(onehot[begin : begin + step, :], source[...]).astype(bf16)
            sbuf[phase, begin // slots : (begin + step) // slots] = picked.reshape(
                step // slots, slots, width
            )
        halo[phase, core, me] = sbuf[phase, me]

    def halo_send(phase):
        def send(i, _):
            q = lax.rem(me + i, parts)
            remote(
                sbuf.at[phase, q],
                halo.at[phase, core, me],
                h_send.at[phase, q],
                h_recv.at[phase, me],
                q,
                core,
            ).start()
            return 0

        lax.fori_loop(1, parts, send, 0)
        forward(phase, me).start()

    def forward(phase, s):
        return remote(
            halo.at[phase, core, s],
            halo.at[phase, core, s],
            f_send.at[phase, s],
            f_recv.at[phase, s],
            me,
            sib,
        )

    def arrival(phase, s):
        return remote(
            sbuf.at[phase, s],
            halo.at[phase, core, s],
            h_send.at[phase, s],
            h_recv.at[phase, s],
            s,
            core,
        )

    def halo_recv(phase):
        def take(i, _):
            s = lax.rem(me + parts - i, parts)
            arrival(phase, s).wait_recv()
            forward(phase, s).start()
            return 0

        lax.fori_loop(1, parts, take, 0)

        def settle(s, _):
            remote(
                halo.at[phase, sib, s],
                halo.at[phase, sib, s],
                f_send.at[phase, s],
                f_recv.at[phase, s],
                me,
                sib,
            ).wait_recv()
            return 0

        lax.fori_loop(0, parts, settle, 0)

    def landed_rows(phase):
        return halo[phase].reshape(2 * own_rows, width)

    halo_pick(0, own_pick, states.at[0])
    pl.semaphore_wait(barrier, parts)
    halo_send(0)

    weight_copies = []
    for k, (src, dst) in enumerate(((wg_in, wg), (wu_in, wu), (wd_in, wd))):
        load_weights[k].wait()
        copy = remote(dst.at[core], dst.at[core], w_send.at[k], w_recv.at[k], me, sib)
        copy.start()
        weight_copies.append(copy)

    load_tiles.wait()
    lay_out(1, targets)

    def build(r, _):
        held = [col_ref[j, r] for j in range(tiles_ref.shape[1])]
        for c in range(blocks):
            j = jnp.int32(-1)
            for k, col in enumerate(held):
                j = jnp.where(col == c, k, j)
            inv_ref[r, c] = j
            tile = tiles_ref[r, jnp.maximum(j, 0)]
            adj[aligned(r, BLOCK), c * BLOCK : (c + 1) * BLOCK] = jnp.where(
                j >= 0, tile, jnp.zeros_like(tile)
            )
        return 0

    lax.fori_loop(0, blocks, build, 0)

    def build_send(i, _):
        at = aligned(i, TILE)
        index = lax.broadcasted_iota(jnp.int32, (TILE, 2 * own_rows), 0) + i * TILE
        s_t[at, :] = (idx_ref[0:1, :] == index).astype(f32).astype(bf16)
        return 0

    def build_receive(i, _):
        at = aligned(i, TILE)
        index = lax.broadcasted_iota(jnp.int32, (TILE, 2 * own_rows), 0) + i * TILE
        r_t[at, :] = (idx_ref[1:2, :] == index).astype(f32).astype(bf16)
        return 0

    def place_turned():
        def turn(r, _):
            for c in range(blocks):
                j = inv_ref[r, c]
                tile = tiles_ref[r, jnp.maximum(j, 0)]
                adj_t[c * BLOCK : (c + 1) * BLOCK, aligned(r, BLOCK)] = jnp.where(
                    j >= 0, tile, jnp.zeros_like(tile)
                )
            return 0

        lax.fori_loop(0, blocks, turn, 0)

    def turn_share(part, whole):
        for r in range(part * blocks // whole, (part + 1) * blocks // whole):
            for j in range(tiles_ref.shape[1]):
                tiles_ref[r, j] = jnp.transpose(tiles_ref[r, j])

    for layer in range(layers):
        if layer:
            halo_pick(layer, own_pick, states.at[layer])
            halo_send(layer)
        state = states.at[layer]

        for begin in range(0, rows, 2 * TILE):
            at = pl.ds(begin, 2 * TILE)
            fg_ref[at, :] = dot_nn(adj[at, :], state[...])
        if layer == 0:
            each_tile(build_receive)
            for copy in weight_copies:
                copy.wait_recv()
        if layer == layers - 1:
            pick_rows(targets)
            lay_out(0, sources)
            each_tile(build_send)
            for plain, turned in ((wg, wg_t), (wu, wu_t), (wd, wd_t)):
                for h in range(2):
                    for k in range(layers):
                        turned[h, k] = jnp.transpose(plain[h, k])
        halo_recv(layer)

        def mlp(i, _, layer=layer, state=state):
            at = aligned(i, TILE)
            turn_share(layer * tiles + i, layers * tiles)
            act = (fg_ref[at, :] + dot_nn(r_t[at, :], landed_rows(layer))).astype(bf16)
            acts_t[layer, :, at] = jnp.transpose(act)
            made = []
            mixed = jnp.zeros((TILE, width), f32)
            for h in range(2):
                gate = dot_nn(act, wg[h, layer])
                up = dot_nn(act, wu[h, layer])
                sg = 0.5 * jnp.tanh(0.5 * gate) + 0.5
                silu = gate * sg
                hidden = (silu * up).astype(bf16)
                made.append(hidden)
                pre_g[layer, h, at, :] = (up * (sg * (1.0 + gate * (1.0 - sg)))).astype(bf16)
                pre_u[layer, h, at, :] = silu.astype(bf16)
                mixed = mixed + dot_nn(hidden, wd[h, layer])
            hid_t[layer, :, at] = jnp.transpose(jnp.where(core == 0, made[0], made[1]))
            new = ((state[at, :].astype(f32) + mixed) * mask_of(i)).astype(bf16)
            if layer + 1 < layers:
                states[layer + 1, at, :] = new
            else:
                final_ref[at, :] = new
            return 0

        each_tile(mlp)

    total = grads.shape[1]
    p_rows = total * 2 // 3
    p_half = p_rows // 2
    p_seg = p_half // outer
    q_seg = (total - p_rows) // outer
    q_half = q_seg // 2

    def at_rows(base, index, size):
        return pl.ds(pl.multiple_of(base + index * size, 16), size)

    def each_other(fn):
        def go(i, _):
            fn(lax.rem(z + i, outer))
            return 0

        lax.fori_loop(1, outer, go, 0)

    def pair(stage, layer, src, dst, slot):
        return remote(
            src,
            dst,
            a_send.at[layer, stage, outer + slot],
            a_recv.at[layer, stage, outer + slot],
            z * 2 + 1 - y,
            core,
        )

    def line(stage, layer, src, dst, to, slot, bank=0):
        return remote(
            src,
            dst,
            a_send.at[layer, stage, bank * outer + to],
            a_recv.at[layer, stage, bank * outer + slot],
            to * 2 + y,
            core,
        )

    def p_first(layer, t):
        return pair(
            0,
            layer,
            grads.at[layer, at_rows((1 - y) * p_half, t, p_seg)],
            p_one.at[layer, at_rows(0, t, p_seg)],
            t,
        )

    def p_added(layer, t):
        mine = grads[layer, at_rows(y * p_half, t, p_seg)].astype(f32)
        return (mine + p_one[layer, at_rows(0, t, p_seg)].astype(f32)).astype(bf16)

    def p_across(layer, t, slot):
        return line(
            1, layer, p_sum.at[layer, at_rows(0, t, p_seg)], p_two.at[layer, slot], t, slot
        )

    def p_spread(layer, owner, t, slot):
        place = res.at[layer, at_rows(y * p_half, owner, p_seg)]
        return line(2, layer, place, place, t, slot)

    def p_last(layer, half, t):
        place = res.at[layer, at_rows(half * p_half, t, p_seg)]
        return pair(3, layer, place, place, t)

    def q_first(layer, t, slot):
        return line(
            0,
            layer,
            grads.at[layer, at_rows(p_rows, t, q_seg)],
            q_one.at[layer, slot],
            t,
            slot,
        )

    def q_across(layer):
        source = q_sum.at[layer, at_rows(0, 1 - y, q_half)]
        return pair(1, layer, source, q_two.at[layer], 0)

    def q_spread(layer, half):
        place = res.at[layer, at_rows(p_rows + z * q_seg, half, q_half)]
        return pair(2, layer, place, place, 0)

    def q_last(layer, owner, half, t, slot, bank):
        place = res.at[layer, at_rows(p_rows + owner * q_seg, half, q_half)]
        return line(3, layer, place, place, t, slot, 2 * bank)

    def reduce_one(layer):
        def send(t):
            p_first(layer, t).start()
            q_first(layer, t, z).start()

        each_other(send)
        p_first(layer, z).start()
        q_one[layer, z] = grads[layer, at_rows(p_rows, z, q_seg)]

    def reduce_two(layer):
        def pass_on(t):
            p_first(layer, t).wait_recv()
            p_sum[layer, at_rows(0, t, p_seg)] = p_added(layer, t)
            p_across(layer, t, z).start()

        each_other(pass_on)
        p_first(layer, z).wait_recv()
        p_two[layer, z] = p_added(layer, z)
        each_other(lambda t: q_first(layer, t, t).wait_recv())
        q_sum[layer] = jnp.sum(q_one[layer].astype(f32), axis=0).astype(bf16)
        q_across(layer).start()

    def reduce_three(layer):
        each_other(lambda t: p_across(layer, t, t).wait_recv())
        res[layer, at_rows(y * p_half, z, p_seg)] = jnp.sum(
            p_two[layer].astype(f32), axis=0
        ).astype(bf16)
        each_other(lambda t: p_spread(layer, z, t, z).start())
        p_last(layer, y, z).start()
        q_across(layer).wait_recv()
        res[layer, at_rows(p_rows + z * q_seg, y, q_half)] = (
            q_sum[layer, at_rows(0, y, q_half)].astype(f32) + q_two[layer].astype(f32)
        ).astype(bf16)
        q_spread(layer, y).start()
        each_other(lambda t: q_last(layer, z, y, t, z, 0).start())

    def reduce_four(layer):
        q_spread(layer, 1 - y).wait_recv()

        def pass_on(t):
            p_spread(layer, t, t, t).wait_recv()
            p_last(layer, y, t).start()
            q_last(layer, z, 1 - y, t, z, 1).start()

        each_other(pass_on)

    def reduce_drain(layer):
        def sent(t):
            p_first(layer, t).wait_send()
            q_first(layer, t, z).wait_send()
            p_across(layer, t, z).wait_send()
            p_spread(layer, z, t, z).wait_send()
            p_last(layer, y, t).wait_send()
            q_last(layer, z, y, t, z, 0).wait_send()
            q_last(layer, z, 1 - y, t, z, 1).wait_send()

        each_other(sent)
        p_first(layer, z).wait_send()
        p_last(layer, y, z).wait_send()
        q_across(layer).wait_send()
        q_spread(layer, y).wait_send()

    def stores(layer):
        return [
            pltpu.make_async_copy(ref.at[layer], out.at[layer], o_sem.at[2 + k, layer])
            for k, (ref, out) in enumerate(((gg_ref, gg_out), (gu_ref, gu_out), (gd_ref, gd_out)))
        ]

    store_final = pltpu.make_async_copy(final_ref, final_out, o_sem.at[0, 0])
    store_final.start()
    store_fg = pltpu.make_async_copy(fg_ref, fg_out, o_sem.at[1, 0])

    def reduce_end(layer):
        def landed(t):
            p_last(layer, 1 - y, t).wait_recv()
            q_last(layer, t, y, t, t, 0).wait_recv()
            q_last(layer, t, 1 - y, t, t, 1).wait_recv()

        each_other(landed)
        p_last(layer, 1 - y, z).wait_recv()
        at = 0
        for out in (gg_ref, gu_ref, gd_ref):
            height, wide = out.shape[1:]
            for c in range(0, wide, LANES):
                out[layer, :, c : c + LANES] = res[layer, at : at + height].astype(f32)
                at += height
        for copy in stores(layer):
            copy.start()

    down_in, agg_grad = states.at[0], states.at[1]
    load_cot.wait()

    def start_rows(i, _):
        at = aligned(i, TILE)
        fg_ref[at, :] = cot_ref[at, :].astype(f32) * mask_of(i)
        return 0

    each_tile(start_rows)

    for layer in reversed(range(layers)):
        phase = 2 * layers - 1 - layer
        last = layer == layers - 1

        def mlp_back(i, _, layer=layer):
            at = aligned(i, TILE)
            down = fg_ref[at, :].astype(bf16)
            down_in[at, :] = down
            for h in range(2):
                hidden_grad = dot_nn(down, wd_t[h, layer])
                gate_grad = (hidden_grad * pre_g[layer, h, at, :].astype(f32)).astype(bf16)
                up_grad = (hidden_grad * pre_u[layer, h, at, :].astype(f32)).astype(bf16)
                pre_g[layer, h, at, :] = gate_grad
                pre_u[layer, h, at, :] = up_grad
            return 0

        def through_weights(i, _, layer=layer):
            at = aligned(i, TILE)
            total = jnp.zeros((TILE, width), f32)
            for h in range(2):
                total = total + dot_nn(pre_g[layer, h, at, :], wg_t[h, layer])
                total = total + dot_nn(pre_u[layer, h, at, :], wu_t[h, layer])
            agg_grad[at, :] = total.astype(bf16)
            return 0

        def weight_gradients(layer=layer):
            at = 0
            act = acts_t[layer]
            for left, right in (
                (act, pre_g[layer, core]),
                (act, pre_u[layer, core]),
                (hid_t[layer], down_in[...]),
            ):
                part = dot_nn(left, right).astype(bf16)
                for c in range(0, part.shape[1], LANES):
                    grads[layer, at : at + part.shape[0], :] = part[:, c : c + LANES]
                    at += part.shape[0]
            reduce_one(layer)

        each_tile(mlp_back)
        if layer == 0:
            weight_gradients()
            if not last:
                reduce_three(layer + 1)
        each_tile(through_weights)
        halo_pick(phase, own_pick, agg_grad)
        halo_send(phase)
        if layer:
            if not last:
                reduce_three(layer + 1)
            weight_gradients()
        if last:
            place_turned()

        for begin in range(0, rows, 2 * TILE):
            at = pl.ds(begin, 2 * TILE)
            fg_ref[at, :] = fg_ref[at, :] + dot_nn(adj_t[at, :], agg_grad[...])
        if not last:
            reduce_two(layer)
        halo_recv(phase)
        if not last:
            reduce_four(layer + 1)

        def finish(i, _, phase=phase):
            at = aligned(i, TILE)
            fg_ref[at, :] = (fg_ref[at, :] + dot_nn(s_t[at, :], landed_rows(phase))) * mask_of(i)
            return 0

        each_tile(finish)
        if last:
            reduce_two(layer)

    store_fg.start()
    reduce_three(0)
    for layer in range(1, layers):
        reduce_end(layer)
    reduce_four(0)
    reduce_end(0)
    store_final.wait()
    store_fg.wait()
    for layer in range(layers):
        reduce_drain(layer)
        for copy in stores(layer):
            copy.wait()
    for copy in weight_copies:
        copy.wait_send()
    for phase in range(2 * layers):

        def drained(i, _, phase=phase):
            q = lax.rem(me + i, parts)
            arrival(phase, q).wait_send()
            forward(phase, q).wait_send()
            return 0

        lax.fori_loop(1, parts, drained, 0)
        forward(phase, me).wait_send()


def hand_over(*refs):
    count = (len(refs) - 2) // 3
    in_sem, out_sem = refs[-2:]
    pairs = []
    for k in range(count):
        source, target, held = refs[k], refs[count + k], refs[2 * count + k]
        cuts = 2 if source.shape[0] < 8 else 4
        size = source.shape[0] // cuts
        for cut in range(cuts):
            at = pl.ds(cut * size, size)
            pairs.append(
                (
                    pltpu.make_async_copy(source.at[at], held.at[at], in_sem.at[k, cut]),
                    pltpu.make_async_copy(held.at[at], target.at[at], out_sem.at[k, cut]),
                )
            )
    for load, _ in pairs:
        load.start()
    for load, store in pairs:
        load.wait()
        store.start()
    for _, store in pairs:
        store.wait()


def local(
    parts,
    feats,
    cell_count,
    tile_col,
    tile_val,
    send_list,
    send_count,
    recv_list,
    gate_weight_matrix,
    w_up,
    w_down,
    out_grad,
):
    rows, width = feats.shape
    layers, _, units = gate_weight_matrix.shape
    slot_count = send_list.shape[2]
    half = slot_count // 2
    outer = parts // 2
    all_slots = parts * slot_count
    total = 2 * width * (units // LANES) + units * (width // LANES)
    p_half = total // 3
    q_seg = (total - 2 * p_half) // outer
    f32, bf16 = jnp.float32, jnp.bfloat16
    vmem = pl.BlockSpec(memory_space=pltpu.VMEM)
    hbm = pl.BlockSpec(memory_space=pl.ANY)
    smem = pl.BlockSpec(memory_space=pltpu.SMEM)
    phases = 2 * layers
    dma = pltpu.SemaphoreType.DMA
    outs = pl.pallas_call(
        functools.partial(kernel, parts),
        out_shape=(
            jax.ShapeDtypeStruct((rows, width), bf16),
            jax.ShapeDtypeStruct((rows, width), f32),
            jax.ShapeDtypeStruct((layers, width, units), f32),
            jax.ShapeDtypeStruct((layers, width, units), f32),
            jax.ShapeDtypeStruct((layers, units, width), f32),
        ),
        in_specs=[smem, smem] + [vmem] * 4 + [hbm] * 5,
        out_specs=[hbm] * 5,
        scratch_shapes=[
            pltpu.VMEM((8, all_slots), jnp.int32),
            pltpu.VMEM(tile_val.shape, bf16),
            pltpu.VMEM((rows, width), bf16),
            pltpu.VMEM((rows, width), bf16),
            pltpu.VMEM((rows, width), f32),
            pltpu.VMEM((layers, width, units), f32),
            pltpu.VMEM((layers, width, units), f32),
            pltpu.VMEM((layers, units, width), f32),
            pltpu.VMEM((rows, rows), bf16),
            pltpu.VMEM((rows, rows), bf16),
            pltpu.VMEM((all_slots // 2, rows), bf16),
            pltpu.VMEM((rows, all_slots), bf16),
            pltpu.VMEM((rows, all_slots), bf16),
            pltpu.VMEM((max(layers, 2), rows, width), bf16),
            pltpu.VMEM((layers, width, rows), bf16),
            pltpu.VMEM((layers, units, rows), bf16),
            pltpu.VMEM((layers, 2, rows, units), bf16),
            pltpu.VMEM((layers, 2, rows, units), bf16),
            pltpu.VMEM((2, layers, width, units), bf16),
            pltpu.VMEM((2, layers, width, units), bf16),
            pltpu.VMEM((2, layers, units, width), bf16),
            pltpu.VMEM((2, layers, units, width), bf16),
            pltpu.VMEM((2, layers, units, width), bf16),
            pltpu.VMEM((2, layers, width, units), bf16),
            pltpu.VMEM((phases, parts, half, width), bf16),
            pltpu.VMEM((phases, 2, parts, half, width), bf16),
            pltpu.VMEM((layers, total, LANES), bf16),
            pltpu.VMEM((layers, total, LANES), bf16),
            pltpu.VMEM((layers, p_half, LANES), bf16),
            pltpu.VMEM((layers, p_half, LANES), bf16),
            pltpu.VMEM((layers, outer, p_half // outer, LANES), bf16),
            pltpu.VMEM((layers, outer, q_seg, LANES), bf16),
            pltpu.VMEM((layers, q_seg, LANES), bf16),
            pltpu.VMEM((layers, q_seg // 2, LANES), bf16),
            dma((phases, parts)),
            dma((phases, parts)),
            dma((phases, parts)),
            dma((phases, parts)),
            dma((3,)),
            dma((3,)),
            dma((layers, 4, 3 * outer)),
            dma((layers, 4, 3 * outer)),
            dma((5,)),
            dma((5, layers)),
            pltpu.SMEM((rows // BLOCK, rows // BLOCK), jnp.int32),
        ],
        compiler_params=pltpu.CompilerParams(
            collective_id=0, has_side_effects=True, vmem_limit_bytes=60 * 1024 * 1024
        ),
        cost_estimate=pl.CostEstimate(
            flops=14 * 10**9, bytes_accessed=12 * 10**6, transcendentals=rows * units * 4
        ),
    )(
        jnp.transpose(tile_col),
        cell_count,
        send_list,
        send_count,
        recv_list,
        feats,
        tile_val,
        out_grad,
        gate_weight_matrix,
        w_up,
        w_down,
    )
    return pl.pallas_call(
        hand_over,
        out_shape=tuple(jax.ShapeDtypeStruct(out.shape, out.dtype) for out in outs),
        in_specs=[hbm] * len(outs),
        out_specs=[hbm] * len(outs),
        scratch_shapes=[pltpu.VMEM(out.shape, out.dtype) for out in outs]
        + [dma((len(outs), 4)), dma((len(outs), 4))],
        compiler_params=pltpu.CompilerParams(vmem_limit_bytes=60 * 1024 * 1024),
    )(*outs)


def solution(mesh):
    return jax.shard_map(
        functools.partial(local, mesh.shape["dom"]),
        mesh=mesh,
        in_specs=(
            P(("groups", "dom"), None),
            P(("groups", "dom")),
            P(("groups", "dom"), None),
            P(("groups", "dom"), None, None, None),
            P(("groups", "dom"), None, None),
            P(("groups", "dom"), None),
            P(("groups", "dom"), None, None),
            P(None, None, "mp"),
            P(None, None, "mp"),
            P(None, "mp", None),
            P(("groups", "dom"), None),
        ),
        out_specs=(
            P(("groups", "dom"), None),
            P(("groups", "dom"), None),
            P("groups", None, "mp"),
            P("groups", None, "mp"),
            P("groups", "mp", None),
        ),
        check_vma=False,
    )
```
